256 devices in a mesh: lat: 16 (over y, x_lo, core), lon: 16 (over x_hi, z).
Axes of the slice: x: 4 (x_hi: 2, x_lo: 2; x = x_hi * 2 + x_lo), y: 4, z: 8, core: 2. Of those that a mesh axis runs over, the one named last changes fastest.
Arguments:
- state: bfloat16 [256, 384, 2048], P(None, 'lat', 'lon'), may hold values from -6 to 6
- obs_values: bfloat16 [64, 524288], P(None, ('lat', 'lon')), may hold values from -6 to 6
- obs_offsets: float32 [2, 524288], P(None, ('lat', 'lon')), may hold values from 0 to 1
- obs_cell: int32 [524288], P(('lat', 'lon')), may hold values from 0 to 3071, as said below
- obs_count: int32 [256], P(('lat', 'lon')), may hold values from 64 to 2048, as said below
- w_in: bfloat16 [65, 256], replicated, may hold values from -0.75 to 0.75
- dw_weight: float32 [256, 7, 7], replicated, may hold values from -0.875 to 0.875
- dw_bias: float32 [256], replicated, may hold values from -3 to 3
- norm_gain: float32 [256], replicated, may hold values from 0.1 to 1.9
- norm_bias: float32 [256], replicated, may hold values from -3 to 3
- w_up: bfloat16 [256, 1024], replicated, may hold values from -0.375 to 0.375
- up_bias: float32 [1024], replicated, may hold values from -3 to 3
- w_down: bfloat16 [1024, 256], replicated, may hold values from -0.1875 to 0.1875
- down_bias: float32 [256], replicated, may hold values from -3 to 3
- layer_scale: float32 [256], replicated, may hold values from 0.1 to 1.9
Outputs:
- result: bfloat16 [256, 384, 2048], P(None, 'lat', 'lon')
The draws below stay inside these ranges and needn't reach their ends.
Inputs may be any that keep to these rules, and one draw needn't show every extreme that they name: obs_cell numbers a cell inside the slot's own tile as row * 128 + column, row below 24 and column below 128, padding slots included; tiles are numbered along latitude first, then longitude, tile t holding latitude rows from 24 * (t // 16) and longitude columns from 128 * (t % 16). The live slots of each tile are its first obs_count slots; the rest are padding.
All inputs are finite; a program needn't handle non-finite values.
Results may differ from the reference program's by a relative error of at most 0.0065.
Values may be sent and summed in bfloat16 or wider, within the bound.
No kernel may reach another device: no remote copies, remote signals or barrier semaphores. Data moves between devices by JAX's collectives and lax.ppermute only.
A program may use at most 128 MiB of HBM per device.

```python
import jax
import jax.numpy as jnp
from jax import lax

C = 256
HID = 1024
SRC = 64
KERNEL = 7
W = 4
CLAT = 24
CLON = 128
OBS_DEV = 2048
LAT = 384
LON = 2048
TILES = 256
NOBS = 524288
N_LON = 16


def draw_obs_cell(key, part):
    row_total = OBS_DEV * TILES
    row_ids = jnp.arange(row_total, dtype=jnp.int32)
    first_key, second_key = jax.random.split(key)
    inner_row = jax.random.randint(first_key, (row_total,), 0, CLAT, dtype=jnp.int32)
    inner_column = jax.random.randint(second_key, (row_total,), 0, CLON, dtype=jnp.int32)
    inner_row = jnp.where(row_ids == 0, 0, inner_row)
    inner_column = jnp.where(row_ids == 0, 0, inner_column)
    last_start = row_total - OBS_DEV
    inner_row = jnp.where(row_ids == last_start, CLAT - 1, inner_row)
    inner_column = jnp.where(row_ids == last_start, CLON - 1, inner_column)
    return (inner_row * CLON + inner_column).astype(jnp.int32)


def draw_obs_count(key, part):
    tiles_lon = LON // CLON
    tiles_lat = LAT // CLAT
    tile_ids = jnp.arange(TILES, dtype=jnp.int32)
    tile_row = tile_ids // tiles_lon
    tile_column = tile_ids % tiles_lon
    key_list = jax.random.split(key, 4)
    swath_shift = jax.random.randint(key_list[0], (), 0, tiles_lon, dtype=jnp.int32)
    swath_width = max(tiles_lon // 4, 1)
    in_swath = (tile_column - swath_shift - tile_row) % tiles_lon < swath_width
    least = max(OBS_DEV // 32, 1)
    heavy = jax.random.randint(key_list[1], (TILES,), OBS_DEV // 2, OBS_DEV + 1, dtype=jnp.int32)
    light = jax.random.randint(key_list[2], (TILES,), least, OBS_DEV // 8 + 1, dtype=jnp.int32)
    counts = jnp.where(in_swath, heavy, light)
    chosen_row = jax.random.randint(key_list[3], (), 0, tiles_lat, dtype=jnp.int32)
    full_tile = chosen_row * tiles_lon + (swath_shift + chosen_row) % tiles_lon
    sparse_tile = chosen_row * tiles_lon + (swath_shift + chosen_row + tiles_lon // 2) % tiles_lon
    counts = jnp.where(tile_ids == full_tile, OBS_DEV, counts)
    counts = jnp.where(tile_ids == sparse_tile, least, counts)
    return counts.astype(jnp.int32)


def shard_levels(stream_key, extent, cuts, low, largest):
    def one(axis_at, parts):
        steps = jax.random.uniform(jax.random.fold_in(jax.random.fold_in(stream_key, 6), axis_at), (parts,), jnp.float32, low / len(cuts), largest / len(cuts))
        return jnp.repeat(jnp.exp(steps), extent[axis_at] // parts).reshape((-1,) + (1,) * (len(extent) - axis_at - 1))

    level = one(*cuts[0])
    for cut in cuts[1:]:
        level = level * one(*cut)
    return level


def gaussian(key, extent, deviation, bound, cuts=(), held_as=jnp.bfloat16):
    factor_of = shard_levels(key, extent, cuts, -0.22, 0.18) if cuts else 1.0
    values = jax.random.normal(key, extent, jnp.float32) * deviation * factor_of
    return jnp.minimum(jnp.maximum(values, -bound), bound).astype(held_as)


def setup_inputs(seed: int = 0) -> dict:
    streams_of = jax.random.split(jax.random.key(seed), 16)
    return {
        "state": gaussian(streams_of[0], (C, LAT, LON), 1.0, 6.0, ((1, 16), (2, 16))),
        "obs_values": gaussian(streams_of[1], (SRC, NOBS), 1.0, 6.0, ((1, 256),)),
        "obs_offsets": jnp.clip(1.0 * jax.random.uniform(streams_of[2], (2, NOBS), jnp.float32) ** shard_levels(streams_of[2], (2, NOBS), ((1, 256),), -0.2, 0.2), 0.0, 1.0),
        "obs_cell": draw_obs_cell(jax.random.fold_in(streams_of[15], 71), 0),
        "obs_count": draw_obs_count(jax.random.fold_in(streams_of[15], 71), 0),
        "w_in": gaussian(streams_of[5], (SRC + 1, C), (SRC + 1) ** -0.5, 0.75),
        "dw_weight": gaussian(streams_of[6], (C, KERNEL, KERNEL), (KERNEL * KERNEL) ** -0.5, 0.875, (), jnp.float32),
        "dw_bias": gaussian(streams_of[7], (C,), 0.5, 3.0, (), jnp.float32),
        "norm_gain": jnp.clip(1.0 + 0.18 * jax.random.normal(streams_of[8], (C,), jnp.float32), 0.1, 1.9),
        "norm_bias": gaussian(streams_of[9], (C,), 0.5, 3.0, (), jnp.float32),
        "w_up": gaussian(streams_of[10], (C, HID), C ** -0.5, 0.375),
        "up_bias": gaussian(streams_of[11], (HID,), 0.5, 3.0, (), jnp.float32),
        "w_down": gaussian(streams_of[12], (HID, C), HID ** -0.5, 0.1875),
        "down_bias": gaussian(streams_of[13], (C,), 0.5, 3.0, (), jnp.float32),
        "layer_scale": jnp.clip(1.0 + 0.18 * jax.random.normal(streams_of[14], (C,), jnp.float32), 0.1, 1.9),
    }


inverse_width = 1.0 / (2.0 * 1.5 * 1.5)

def reference(state, obs_values, obs_offsets, obs_cell, obs_count, w_in, dw_weight, dw_bias, norm_gain, norm_bias, w_up, up_bias, w_down, down_bias, layer_scale):
    row_total = obs_cell.shape[0]
    row_ids = jnp.arange(row_total, dtype=jnp.int32)
    tile_ids = row_ids // OBS_DEV
    live_rows = row_ids % OBS_DEV < obs_count[tile_ids]
    lat_cells = tile_ids // N_LON * CLAT + obs_cell // CLON
    lon_cells = tile_ids % N_LON * CLON + obs_cell % CLON
    values_rows = obs_values.T.astype(jnp.float32)
    span = 2 * W + 1

    def reach_step(number, running):
        sums, density = running
        lat_shift = number // span - W
        lon_shift = number % span - W
        target_lat = lat_cells + lat_shift
        inside = live_rows & (target_lat >= 0) & (target_lat < LAT)
        lat_spread = obs_offsets[0] - lat_shift.astype(jnp.float32) - 0.5
        lon_spread = obs_offsets[1] - lon_shift.astype(jnp.float32) - 0.5
        lat_weight = jnp.where(inside, jnp.exp(-lat_spread * lat_spread * inverse_width), 0.0)
        lon_weight = jnp.exp(-lon_spread * lon_spread * inverse_width)
        scaled = lax.optimization_barrier((values_rows * lat_weight[:, None]).astype(jnp.bfloat16)).astype(jnp.float32)
        lon_narrow = lax.optimization_barrier(lon_weight.astype(jnp.bfloat16)).astype(jnp.float32)
        target = jnp.where(inside, target_lat * LON + (lon_cells + lon_shift) % LON, 0).astype(jnp.int32)
        sums = sums.at[target].add(scaled * lon_narrow[:, None])
        density = density.at[target].add(lat_weight * lon_weight)
        return (sums, density)
    start_sums = jnp.zeros((LAT * LON, SRC), jnp.float32)
    start_density = jnp.zeros((LAT * LON,), jnp.float32)
    sums, density = lax.fori_loop(0, span * span, reach_step, (start_sums, start_density))
    sources = jnp.concatenate([sums.T, density[None, :]], 0).reshape(SRC + 1, LAT, LON).astype(jnp.bfloat16)
    blocks = LAT // CLAT
    block_ids = jnp.arange(blocks, dtype=jnp.int32)

    def encode_block(number):
        piece = lax.dynamic_slice_in_dim(sources, number * CLAT, CLAT, 1).reshape(SRC + 1, CLAT * LON)
        base = lax.dynamic_slice_in_dim(state, number * CLAT, CLAT, 1).reshape(C, CLAT * LON)
        projected = jnp.dot(w_in.T, piece, preferred_element_type=jnp.float32)
        return (base.astype(jnp.float32) + projected).astype(jnp.bfloat16).reshape(C, CLAT, LON)
    mixed = lax.map(encode_block, block_ids)
    mixed = jnp.transpose(mixed, (1, 0, 2, 3)).reshape(C, LAT, LON)
    half = KERNEL // 2
    wrapped = jnp.concatenate([mixed[:, :, LON - half:], mixed, mixed[:, :, :half]], 2)
    padded = jnp.pad(wrapped, ((0, 0), (half, half), (0, 0)))

    def layer_block(number):
        window = lax.dynamic_slice_in_dim(padded, number * CLAT, CLAT + 2 * half, 1)
        filtered = jnp.zeros((C, CLAT, LON), jnp.float32) + dw_bias[:, None, None]
        for shift_row in range(KERNEL):
            for shift_col in range(KERNEL):
                filtered = filtered + window[:, shift_row:shift_row + CLAT, shift_col:shift_col + LON].astype(jnp.float32) * dw_weight[:, shift_row, shift_col][:, None, None]
        centre = filtered - lax.optimization_barrier(jnp.mean(filtered, axis=0, keepdims=True))
        spread = lax.optimization_barrier(jnp.mean(centre * centre, axis=0, keepdims=True))
        normed = (centre * lax.rsqrt(spread + 1e-06) * norm_gain[:, None, None] + norm_bias[:, None, None]).astype(jnp.bfloat16)
        flat = normed.reshape(C, CLAT * LON)
        hidden = jax.nn.gelu(jnp.dot(w_up.T, flat, preferred_element_type=jnp.float32) + up_bias[:, None], approximate=False).astype(jnp.bfloat16)
        update = jnp.dot(w_down.T, hidden, preferred_element_type=jnp.float32) + down_bias[:, None]
        centre_rows = window[:, half:half + CLAT, half:half + LON].astype(jnp.float32)
        return (centre_rows + layer_scale[:, None, None] * update.reshape(C, CLAT, LON)).astype(jnp.bfloat16)
    result = lax.map(layer_block, block_ids)
    return jnp.transpose(result, (1, 0, 2, 3)).reshape(C, LAT, LON)
```

```python
import jax
import jax.numpy as jnp
from jax import lax
from jax.experimental import pallas as pl
from jax.experimental.pallas import tpu as pltpu
from jax.sharding import PartitionSpec as P

KERNEL = 7
W = 4
BLOCK = 128


inverse_width = 1.0 / (2.0 * 1.5 * 1.5)


def with_halo(x, sides, width, wrap):
    for axis, dim in sides:
        size, length = (lax.axis_size(axis), x.shape[dim])
        up = [(i, (i + 1) % size) for i in range(size if wrap else size - 1)]
        down = [(j, i) for i, j in up]
        last = lax.slice_in_dim(x, length - width, length, axis=dim)
        initial = lax.slice_in_dim(x, 0, width, axis=dim)
        before = lax.ppermute(last, axis, up)
        after = lax.ppermute(initial, axis, down)
        x = jnp.concatenate([before, x, after], axis=dim)
    return x


def gaussian_rows(offset, cell_index, extent, base, live_rows):
    places = lax.broadcasted_iota(jnp.int32, (extent, cell_index.shape[0]), 0) - base
    apart = places - cell_index[None, :]
    inside = (jnp.abs(apart) <= W) & live_rows[None, :]
    spread = offset[None, :] - apart.astype(jnp.float32) - 0.5
    return jnp.where(inside, jnp.exp(-spread * spread * inverse_width), 0.0)


def accumulate(packed, live_count, ext_rows, ext_cols, base):
    channels_in = packed.shape[0] - 5
    live_blocks = (live_count + BLOCK - 1) // BLOCK

    def add_block(number, running):
        weighted, density = running
        row_start = number * BLOCK
        piece = lax.dynamic_slice_in_dim(packed, row_start, BLOCK, 1)
        values = piece[:channels_in]
        lat_cells = piece[channels_in + 2].astype(jnp.int32)
        lon_cells = piece[channels_in + 3].astype(jnp.int32)
        live_rows = row_start + lax.iota(jnp.int32, BLOCK) < live_count
        lat_weight = gaussian_rows(piece[channels_in], lat_cells, ext_rows, base, live_rows)
        lon_weight = gaussian_rows(piece[channels_in + 1], lon_cells, ext_cols, base, live_rows)
        scaled = (values[:, None, :] * lat_weight[None, :, :]).astype(jnp.bfloat16)
        scaled = scaled.reshape(channels_in * ext_rows, BLOCK)
        contract = (((1,), (1,)), ((), ()))
        weighted = weighted + lax.dot_general(
            scaled, lon_weight.astype(jnp.bfloat16), contract, preferred_element_type=jnp.float32
        )
        density = density + lax.dot_general(
            lat_weight,
            lon_weight,
            contract,
            precision=lax.Precision.HIGHEST,
            preferred_element_type=jnp.float32,
        )
        return (weighted, density)

    start_weighted = jnp.zeros((channels_in * ext_rows, ext_cols), jnp.float32)
    start_density = jnp.zeros((ext_rows, ext_cols), jnp.float32)
    weighted, density = lax.fori_loop(0, live_blocks, add_block, (start_weighted, start_density))
    return jnp.concatenate(
        [weighted.reshape(channels_in, ext_rows, ext_cols), density[None, :, :]], 0
    )


def observation_sums(obs_values, obs_offsets, obs_cell, obs_count, rows_tile, cols_tile):
    slots = obs_cell.shape[0]
    live_count = obs_count[0]
    live_flag = (lax.iota(jnp.int32, slots) < live_count).astype(jnp.float32)
    own_rows = jnp.concatenate(
        [
            obs_values.astype(jnp.float32),
            obs_offsets,
            (obs_cell // cols_tile).astype(jnp.float32)[None, :],
            (obs_cell % cols_tile).astype(jnp.float32)[None, :],
            live_flag[None, :],
        ],
        0,
    )
    ext_rows = rows_tile + 2 * W
    ext_cols = cols_tile + 2 * W
    partial_value = accumulate(own_rows, live_count, ext_rows, ext_cols, W)
    beside = with_halo(partial_value.astype(jnp.bfloat16), (("lon", 2),), W, True).astype(
        partial_value.dtype
    )
    folded = jnp.concatenate(
        [
            partial_value[:, :, W : 2 * W] + beside[:, :, :W],
            partial_value[:, :, 2 * W : cols_tile],
            partial_value[:, :, cols_tile : cols_tile + W] + beside[:, :, ext_cols + W :],
        ],
        2,
    )
    lat_rims = with_halo(folded.astype(jnp.bfloat16), (("lat", 1),), W, False).astype(folded.dtype)
    gathered = jnp.concatenate(
        [
            folded[:, W : 2 * W, :] + lat_rims[:, :W, :],
            folded[:, 2 * W : rows_tile, :],
            folded[:, rows_tile : rows_tile + W, :] + lat_rims[:, ext_rows + W :, :],
        ],
        1,
    )
    return gathered.astype(jnp.bfloat16)


def encode(sources, state, w_in):
    projected = jnp.einsum("spq,sc->cpq", sources, w_in, preferred_element_type=jnp.float32)
    return (state.astype(jnp.float32) + projected).astype(jnp.bfloat16)


BF = jnp.bfloat16
F = jnp.float32
CB=16
RB=4

def shift_matrix():
    lane = lax.broadcasted_iota(jnp.int32,(256,768),0)
    out = lax.broadcasted_iota(jnp.int32,(256,768),1)
    col = jnp.where(lane<128, lane, jnp.where(lane<132, lane-132, lane-4))
    k = out//128
    d = jnp.where(k<3, k-3, k-2)
    return jnp.where((col == out%128 + d) & (lane<136), 1.0, 0.0).astype(BF)

def block_kernel(dwb, gain, nbias, db, ls, mixed, toe, w1, b1, w2, out, xs, filt, xbuf, obuf, smat):
    f32=jnp.float32
    smat[...] = shift_matrix()
    def filt_step(i, s1):
        c0 = i*CB
        m = mixed[pl.ds(c0,CB)].reshape(CB*32,256)
        for j in range(3):
            z = jnp.dot(m, smat[:, j*256:(j+1)*256], preferred_element_type=f32).astype(BF)
            for hf in range(2):
                k = 2*j+hf
                v = k if k<3 else k+1
                zz = z[:, hf*128:(hf+1)*128]
                for c in range(CB):
                    xs[c//2, v*32:(v+1)*32, (c%2)*128:(c%2)*128+128] = zz[c*32:(c+1)*32]
        for c in range(CB):
            xs[c//2, 96:128, (c%2)*128:(c%2)*128+128] = m[c*32:(c+1)*32,:128]
        for k in range(CB//2):
            o = jnp.dot(toe[i*(CB//2)+k], xs[k], preferred_element_type=f32)
            a = o[:24,:128] + dwb[c0+2*k]
            b = o[24:,128:] + dwb[c0+2*k+1]
            filt[c0+2*k] = a
            filt[c0+2*k+1] = b
            s1 = s1 + (a + b)
        return s1
    s1 = lax.fori_loop(0,256//CB,filt_step,jnp.zeros((24,128),f32))
    mean = s1*(1.0/256)
    def var_step(i, s2):
        for k in range(16):
            a = filt[i*16+k]-mean
            s2 = s2 + a*a
        return s2
    s2 = lax.fori_loop(0,16,var_step,jnp.zeros((24,128),f32))
    rstd = lax.rsqrt(s2*(1.0/256)+1e-6)
    def norm_step(i,_):
        c0=i*16
        ys=[]
        for k in range(16):
            ys.append(((filt[c0+k]-mean)*rstd)*gain[c0+k]+nbias[c0+k])
        y = jnp.stack(ys,0)
        xbuf[:, pl.ds(pl.multiple_of(c0,16),16), :] = jnp.swapaxes(y,0,1).astype(BF)
        return 0
    lax.fori_loop(0,16,norm_step,0)
    def mlp_step(i,_):
        x = jnp.concatenate([xbuf[i*RB+k] for k in range(RB)],1)
        h = jnp.dot(w1[...], x, preferred_element_type=f32)
        gs = []
        for k in range(8):
            hk = h[k*128:(k+1)*128] + b1[:, k:k+1]
            gs.append(((0.5*hk)*(1.0+lax.erf(hk*0.7071067811865476))).astype(BF))
        g = jnp.concatenate(gs, 0)
        o = jnp.dot(w2[...], g, preferred_element_type=f32)
        for k in range(RB):
            obuf[i*RB+k] = o[:,k*128:(k+1)*128]
        return 0
    lax.fori_loop(0,24//RB,mlp_step,0)
    def out_step(i,_):
        c0=pl.multiple_of(i*16,16)
        o = jnp.swapaxes(obuf[:, pl.ds(c0,16), :],0,1)
        m = mixed[pl.ds(c0,16), 4:28, :128].astype(f32)
        for k in range(16):
            out[c0+k] = (m[k] + (o[k] + db[c0+k])*ls[c0+k]).astype(BF)
        return 0
    lax.fori_loop(0,16,out_step,0)


def prepare_kernel(base, w_up, w_down, b1, toe, w1, w2, b1c):
    w1[...] = w_up[...].T
    w2[...] = w_down[...].T
    b1c[...] = b1[...].T
    def step(i,_):
        rows = base[pl.ds(pl.multiple_of(i*8,8),8), :]
        for k in range(8):
            parts=[]
            for ln in range(2):
                b = jnp.broadcast_to(rows[k:k+1, ln*128:(ln+1)*128],(24,128))
                parts.append(pltpu.roll(b, 0, 1, stride=1, stride_axis=0))
            y = jnp.concatenate(parts,1).astype(BF)
            toe[i*4+k//2, (k%2)*24:(k%2)*24+24, :] = y[:, :224]
        return 0
    lax.fori_loop(0,32,step,0)


def prepare(dw_weight, w_up, w_down, up_bias):
    base = jnp.pad(jnp.swapaxes(dw_weight,1,2), ((0,0),(0,1),(1,24))).reshape(256,256)
    S = jax.ShapeDtypeStruct
    return pl.pallas_call(prepare_kernel, name="prepare",
        out_shape=(S((128,48,224),BF), S((1024,256),BF), S((256,1024),BF), S((128,8),F)),
        compiler_params=pltpu.CompilerParams(vmem_limit_bytes=40*2**20))(base, w_up, w_down, up_bias.reshape(8,128))


def block(mixed, toe, w1, w2, b1, dw_bias, norm_gain, norm_bias, down_bias, layer_scale):
    S=pl.BlockSpec(memory_space=pltpu.SMEM)
    V=pl.BlockSpec(memory_space=pltpu.VMEM)
    return pl.pallas_call(block_kernel, out_shape=jax.ShapeDtypeStruct((256,24,128),BF), name="block",
        in_specs=[S]*5+[V]*5, out_specs=V,
        scratch_shapes=[pltpu.VMEM((CB//2,224,256),BF), pltpu.VMEM((256,24,128),F), pltpu.VMEM((24,256,128),BF), pltpu.VMEM((24,256,128),F), pltpu.VMEM((256,768),BF)],
        compiler_params=pltpu.CompilerParams(vmem_limit_bytes=58*2**20))(
        dw_bias, norm_gain, norm_bias, down_bias, layer_scale, mixed, toe, w1, b1, w2)


def local(
    state,
    obs_values,
    obs_offsets,
    obs_cell,
    obs_count,
    w_in,
    dw_weight,
    dw_bias,
    norm_gain,
    norm_bias,
    w_up,
    up_bias,
    w_down,
    down_bias,
    layer_scale,
):
    channels, rows_tile, cols_tile = state.shape
    margin = KERNEL // 2
    sources = observation_sums(obs_values, obs_offsets, obs_cell, obs_count, rows_tile, cols_tile)
    mixed = encode(sources, state, w_in)
    mixed_wide = with_halo(mixed, (("lon", 2),), margin, True)
    padded = with_halo(mixed_wide, (("lat", 1),), margin, False)
    z = lambda n, m: jnp.zeros((channels, n, m), BF)
    body = jnp.concatenate([padded[:, :, margin:-margin], z(rows_tile+6, 1), padded[:, :, :margin], padded[:, :, -margin:], z(rows_tile+6, 121)], 2)
    body = jnp.pad(body, ((0,0),(1,1),(0,0)))
    toe, w1, w2, b1 = prepare(dw_weight, w_up, w_down, up_bias)
    return block(body, toe, w1, w2, b1, dw_bias, norm_gain, norm_bias, down_bias, layer_scale)


def solution(mesh):
    return jax.shard_map(
        local,
        mesh=mesh,
        in_specs=(
            P(None, "lat", "lon"),
            P(None, ("lat", "lon")),
            P(None, ("lat", "lon")),
            P(("lat", "lon")),
            P(("lat", "lon")),
            P(),
            P(),
            P(),
            P(),
            P(),
            P(),
            P(),
            P(),
            P(),
            P(),
        ),
        out_specs=P(None, "lat", "lon"),
        check_vma=False,
    )
```

```python
import jax
import jax.numpy as jnp
from jax import lax
from jax.experimental import pallas as pl
from jax.experimental.pallas import tpu as pltpu
from jax.sharding import PartitionSpec as P

W = 4
SRC = 80
ROWS = 32
OBS_BLOCK = 512
GRID_ROWS = 384
CB = 16
RB = 4
BF = jnp.bfloat16
F = jnp.float32
MIB = 2**20
LAT_STATE = 9 * SRC
LAT_MSG = 9 * SRC + 3 * 256
LON_STATE = 2 * SRC
LON_MSG = 2 * SRC + 2 * 256

inverse_width = 1.0 / (2.0 * 1.5 * 1.5)


def lanes(rows):
    return lax.broadcasted_iota(jnp.int32, (rows, 128), 1)


def sums_kernel(count, row_base, vals, offs, cell, state, sums, up, down, scaled, acc):
    live_count = count[0]
    acc[...] = jnp.zeros(acc.shape, F)

    def add_block(b, _):
        k0 = pl.multiple_of(b * OBS_BLOCK, OBS_BLOCK)
        ks = pl.ds(k0, OBS_BLOCK)
        where_cell = cell[:, ks]
        row = where_cell >> 7
        col = where_cell & 127
        slot = lax.broadcasted_iota(jnp.int32, (1, OBS_BLOCK), 1) + k0
        row = jnp.where(slot < live_count, row, -100)

        def weight(offset, place, centre, valid):
            apart = place - centre
            spread = offset - apart.astype(F) - 0.5
            inside = (jnp.abs(apart) <= W) & valid
            return jnp.where(inside, jnp.exp(-spread * spread * inverse_width), 0.0)

        place = lax.broadcasted_iota(jnp.int32, (ROWS, OBS_BLOCK), 0) - W
        on_grid = (place + row_base[0] >= 0) & (place + row_base[0] < GRID_ROWS)
        lat_weight = weight(offs[0:1, ks], place, row, on_grid)
        place = lax.broadcasted_iota(jnp.int32, (136, OBS_BLOCK), 0)
        first = weight(offs[1:2, ks], place, col, place < 128 + W)
        place = lax.broadcasted_iota(jnp.int32, (8, OBS_BLOCK), 0) - 8
        last = weight(offs[1:2, ks], place, col, place >= -W)
        lon_weight = jnp.concatenate([first, jnp.zeros((112, OBS_BLOCK), F), last], 0).astype(BF)
        ones = jnp.where(lax.broadcasted_iota(jnp.int32, (SRC - 64, OBS_BLOCK), 0) == 0, 1.0, 0.0)
        v = jnp.concatenate([vals[:, ks].astype(F), ones], 0)
        for p in range(ROWS):
            scaled[p * SRC:(p + 1) * SRC] = (v * lat_weight[p:p + 1]).astype(BF)
        for m in range(0, ROWS * SRC, 640):
            acc[m:m + 640] += lax.dot_general(
                scaled[m:m + 640], lon_weight, (((1,), (1,)), ((), ())), preferred_element_type=F)
        return 0

    lax.fori_loop(0, (live_count + OBS_BLOCK - 1) // OBS_BLOCK, add_block, 0)
    for p in range(ROWS):
        sums[p] = acc[p * SRC:(p + 1) * SRC].astype(BF)
    for msg, first, state_tile, state_row in ((up, 0, 0, 0), (down, 24, 16, 5)):
        side = jnp.zeros((SRC, 128), F)
        for i in range(8):
            part = acc[(first + i) * SRC:(first + i + 1) * SRC]
            msg[i * SRC:(i + 1) * SRC] = part[:, :128].astype(BF)
            moved = pltpu.roll(part[:, 128:], i * 8 + 4, 1)
            side = jnp.where((lanes(SRC) >> 3) == i, moved, side)
        msg[8 * SRC:9 * SRC] = side.astype(BF)
        for c in range(0, 256, 16):
            x = jnp.swapaxes(state[c:c + 16, state_tile:state_tile + 8, :].astype(F), 0, 1).astype(BF)
            for j in range(3):
                msg[LAT_STATE + j * 256 + c:LAT_STATE + j * 256 + c + 16] = x[state_row + j]


def observation_sums(obs_values, obs_offsets, obs_cell, obs_count, row_base, state):
    S = pl.BlockSpec(memory_space=pltpu.SMEM)
    V = pl.BlockSpec(memory_space=pltpu.VMEM)
    shape = jax.ShapeDtypeStruct
    return pl.pallas_call(
        sums_kernel, name="observation_sums",
        out_shape=(shape((ROWS, SRC, 256), BF), shape((LAT_MSG, 128), BF), shape((LAT_MSG, 128), BF)),
        in_specs=[S, S] + [V] * 4, out_specs=(V,) * 3,
        scratch_shapes=[pltpu.VMEM((ROWS * SRC, OBS_BLOCK), BF), pltpu.VMEM((ROWS * SRC, 256), F)],
        compiler_params=pltpu.CompilerParams(vmem_limit_bytes=32 * MIB),
    )(obs_count, row_base, obs_values, obs_offsets, obs_cell.reshape(1, -1), state)


def rows_kernel(state, rows, rims):
    def turn(i, _):
        c0 = pl.multiple_of(i * 16, 16)
        rows[:, pl.ds(c0, 16), :] = jnp.swapaxes(state[pl.ds(c0, 16)].astype(F), 0, 1).astype(BF)
        return 0

    lax.fori_loop(0, 16, turn, 0)
    for c in range(0, 256, 64):
        packed = [jnp.zeros((64, 128), F) for _ in range(2)]
        for r in range(24):
            p = r + W
            moved = pltpu.roll(rows[r, c:c + 64, :].astype(F), (p % 16) * 8 + 4, 1)
            packed[p // 16] = jnp.where((lanes(64) >> 3) == p % 16, moved, packed[p // 16])
        for k in range(2):
            rims[k * 256 + c:k * 256 + c + 64] = packed[k].astype(BF)


def state_rows(state):
    shape = jax.ShapeDtypeStruct
    return pl.pallas_call(
        rows_kernel, name="state_rows", out_shape=(shape((24, 256, 128), BF), shape((512, 128), BF)),
        cost_estimate=pl.CostEstimate(flops=10**7, bytes_accessed=8 * 10**6, transcendentals=0),
        compiler_params=pltpu.CompilerParams(vmem_limit_bytes=16 * MIB),
    )(state)


def edge_kernel(sums, rims, above, below, edge, left, right):
    lane = lanes(SRC)
    outer = (lane < 4) | (lane >= 124)
    packed = [[jnp.zeros((SRC, 128), F) for _ in range(2)] for _ in range(2)]
    for p in range(ROWS):
        main = sums[p, :, :128].astype(F)
        side = sums[p, :, 128:].astype(F)
        if p < 8 or p >= 24:
            msg, i, e = (above, p, p) if p < 8 else (below, p - 24, p - 16)
            main = main + msg[i * SRC:(i + 1) * SRC].astype(F)
            moved = pltpu.roll(msg[8 * SRC:9 * SRC].astype(F), 124 - i * 8, 1)
            side = side + jnp.where(outer, moved, 0.0)
            edge[e, :, :128] = main.astype(BF)
            edge[e, :, 128:] = side.astype(BF)
        k, shift = p // 16, (p % 16) * 8 + 4
        here = (lane >> 3) == p % 16
        packed[0][k] = jnp.where(here, pltpu.roll(jnp.where(lane < 4, main, side), shift, 1), packed[0][k])
        packed[1][k] = jnp.where(here, pltpu.roll(jnp.where(lane >= 124, main, side), shift, 1), packed[1][k])
    for k in range(2):
        left[k * SRC:(k + 1) * SRC] = packed[0][k].astype(BF)
        right[k * SRC:(k + 1) * SRC] = packed[1][k].astype(BF)
    for c in range(0, 256, 64):
        for k, msg, first in ((0, above, 1), (1, below, 28)):
            out = rims[k * 256 + c:k * 256 + c + 64].astype(F)
            for j in range(3):
                p = first + j
                x = msg[LAT_STATE + j * 256 + c:LAT_STATE + j * 256 + c + 64].astype(F)
                out = jnp.where((lanes(64) >> 3) == p % 16, pltpu.roll(x, (p % 16) * 8 + 4, 1), out)
            at = LON_STATE + k * 256 + c
            left[at:at + 64] = out.astype(BF)
            right[at:at + 64] = out.astype(BF)


def edge_sums(sums, rims, above, below):
    shape = jax.ShapeDtypeStruct
    return pl.pallas_call(
        edge_kernel, name="edge_sums",
        out_shape=(shape((16, SRC, 256), BF), shape((LON_MSG, 128), BF), shape((LON_MSG, 128), BF)),
        compiler_params=pltpu.CompilerParams(vmem_limit_bytes=16 * MIB),
    )(sums, rims, above, below)


def prepare_kernel(base, w_in, w_up, w_down, b1, toe, wi, w1, w2, b1c):
    wi[...] = w_in[...].astype(F).T.astype(BF)
    w1[...] = w_up[...].T
    w2[...] = w_down[...].T
    b1c[...] = b1[...].T

    def step(i, _):
        rows = base[pl.ds(pl.multiple_of(i * 8, 8), 8), :]
        for k in range(8):
            parts = []
            for ln in range(2):
                b = jnp.broadcast_to(rows[k:k + 1, ln * 128:(ln + 1) * 128], (24, 128))
                parts.append(pltpu.roll(b, 0, 1, stride=1, stride_axis=0))
            y = jnp.concatenate(parts, 1).astype(BF)
            toe[i * 4 + k // 2, (k % 2) * 24:(k % 2) * 24 + 24, :] = y[:, :224]
        return 0

    lax.fori_loop(0, 32, step, 0)


def prepare(dw_weight, w_in, w_up, w_down, up_bias):
    base = jnp.pad(jnp.swapaxes(dw_weight, 1, 2), ((0, 0), (0, 1), (1, 24))).reshape(256, 256)
    shape = jax.ShapeDtypeStruct
    return pl.pallas_call(
        prepare_kernel, name="prepare",
        out_shape=(shape((128, 48, 224), BF), shape((256, SRC), BF), shape((1024, 256), BF), shape((256, 1024), BF), shape((128, 8), F)),
        cost_estimate=pl.CostEstimate(flops=10**7, bytes_accessed=8 * 10**6, transcendentals=0),
        compiler_params=pltpu.CompilerParams(vmem_limit_bytes=24 * MIB),
    )(base, jnp.pad(w_in, ((0, SRC - 65), (0, 0))), w_up, w_down, up_bias.reshape(8, 128))


def shift_matrix():
    lane = lax.broadcasted_iota(jnp.int32, (256, 768), 0)
    out = lax.broadcasted_iota(jnp.int32, (256, 768), 1)
    col = jnp.where(lane < 132, lane, jnp.where(lane >= 252, lane - 256, -1000))
    k = out // 128
    d = jnp.where(k < 3, k - 3, k - 2)
    return jnp.where(col == out % 128 + d, 1.0, 0.0).astype(BF)


def block_kernel(dwb, gain, nbias, db, ls, sums, edge, above, below, rows, left, right, toe, wi, w1, b1, w2, out,
                 mixed, native, xs, filt, xbuf, obuf, smat):
    smat[...] = shift_matrix()
    lane = lanes(SRC)
    low, high = lane < 4, lane >= 124
    wide = lanes(256)
    outer = (wide < 4) | (wide >= 124)

    def encode(p, main, side, state):
        k, shift = p // 16, (124 - (p % 16) * 8) % 128
        at = pl.ds(pl.multiple_of(k * SRC, SRC), SRC)
        a = pltpu.roll(left[at].astype(F), shift, 1)
        b = pltpu.roll(right[at].astype(F), shift, 1)
        main = main.astype(F) + jnp.where(low, a, jnp.where(high, b, 0.0))
        side = side.astype(F) + jnp.where(high, a, jnp.where(low, b, 0.0))
        src = jnp.concatenate([main, side], 1).astype(BF)
        both = jnp.dot(wi[...], src, preferred_element_type=F)
        at = pl.ds(pl.multiple_of(LON_STATE + k * 256, 32), 256)
        rim = jnp.where((wide & 7) < 4, left[at].astype(F), right[at].astype(F))
        rim = jnp.where(outer, pltpu.roll(rim, shift, 1), 0.0)
        mixed[p, :, :128] = (both[:, :128] + state.astype(F)).astype(BF)
        mixed[p, :, 128:] = (both[:, 128:] + rim).astype(BF)

    def halo_row(j, _):
        at = pl.ds(pl.multiple_of(LAT_STATE + j * 256, 16), 256)
        encode(1 + j, edge[1 + j, :, :128], edge[1 + j, :, 128:], above[at])
        encode(28 + j, edge[12 + j, :, :128], edge[12 + j, :, 128:], below[at])
        return 0

    def edge_row(j, _):
        encode(4 + j, edge[4 + j, :, :128], edge[4 + j, :, 128:], rows[j])
        encode(24 + j, edge[8 + j, :, :128], edge[8 + j, :, 128:], rows[20 + j])
        return 0

    def inner_row(j, _):
        encode(8 + j, sums[8 + j, :, :128], sums[8 + j, :, 128:], rows[4 + j])
        return 0

    mixed[0] = jnp.zeros((256, 256), BF)
    mixed[31] = jnp.zeros((256, 256), BF)
    lax.fori_loop(0, 3, halo_row, 0)
    lax.fori_loop(0, 4, edge_row, 0)
    lax.fori_loop(0, 16, inner_row, 0)

    def filt_step(i, s1):
        c0 = pl.multiple_of(i * CB, CB)
        turned = jnp.swapaxes(mixed[:, pl.ds(c0, CB), :].astype(F), 0, 1).astype(BF)
        native[pl.ds(c0, CB)] = turned[:, :, :128]
        m = turned.reshape(CB * ROWS, 256)
        for j in range(3):
            z = jnp.dot(m, smat[:, j * 256:(j + 1) * 256], preferred_element_type=F).astype(BF)
            for half in range(2):
                k = 2 * j + half
                v = k if k < 3 else k + 1
                zz = z[:, half * 128:(half + 1) * 128]
                for c in range(CB):
                    xs[c // 2, v * 32:(v + 1) * 32, (c % 2) * 128:(c % 2) * 128 + 128] = zz[c * 32:(c + 1) * 32]
        for c in range(CB):
            xs[c // 2, 96:128, (c % 2) * 128:(c % 2) * 128 + 128] = m[c * 32:(c + 1) * 32, :128]
        for k in range(CB // 2):
            o = jnp.dot(toe[i * (CB // 2) + k], xs[k], preferred_element_type=F)
            a = o[:24, :128] + dwb[c0 + 2 * k]
            b = o[24:, 128:] + dwb[c0 + 2 * k + 1]
            filt[c0 + 2 * k] = a
            filt[c0 + 2 * k + 1] = b
            s1 = s1 + (a + b)
        return s1

    s1 = lax.fori_loop(0, 256 // CB, filt_step, jnp.zeros((24, 128), F))
    mean = s1 * (1.0 / 256)

    def var_step(i, s2):
        for k in range(16):
            a = filt[i * 16 + k] - mean
            s2 = s2 + a * a
        return s2

    s2 = lax.fori_loop(0, 16, var_step, jnp.zeros((24, 128), F))
    rstd = lax.rsqrt(s2 * (1.0 / 256) + 1e-6)

    def norm_step(i, _):
        c0 = pl.multiple_of(i * 16, 16)
        ys = [((filt[c0 + k] - mean) * rstd) * gain[c0 + k] + nbias[c0 + k] for k in range(16)]
        xbuf[:, pl.ds(c0, 16), :] = jnp.swapaxes(jnp.stack(ys, 0), 0, 1).astype(BF)
        return 0

    lax.fori_loop(0, 16, norm_step, 0)

    def mlp_step(i, _):
        x = jnp.concatenate([xbuf[i * RB + k] for k in range(RB)], 1)
        h = jnp.dot(w1[...], x, preferred_element_type=F)
        gs = []
        for k in range(8):
            hk = h[k * 128:(k + 1) * 128] + b1[:, k:k + 1]
            gs.append(((0.5 * hk) * (1.0 + lax.erf(hk * 0.7071067811865476))).astype(BF))
        o = jnp.dot(w2[...], jnp.concatenate(gs, 0), preferred_element_type=F)
        for k in range(RB):
            obuf[i * RB + k] = o[:, k * 128:(k + 1) * 128]
        return 0

    lax.fori_loop(0, 24 // RB, mlp_step, 0)

    def out_step(i, _):
        c0 = pl.multiple_of(i * 16, 16)
        o = jnp.swapaxes(obuf[:, pl.ds(c0, 16), :], 0, 1)
        m = native[pl.ds(c0, 16)].astype(F)
        for k in range(16):
            out[c0 + k] = (m[k, 4:28] + (o[k] + db[c0 + k]) * ls[c0 + k]).astype(BF)
        return 0

    lax.fori_loop(0, 16, out_step, 0)


def block(arrays, vectors):
    S = pl.BlockSpec(memory_space=pltpu.SMEM)
    V = pl.BlockSpec(memory_space=pltpu.VMEM)
    return pl.pallas_call(
        block_kernel, name="block", out_shape=jax.ShapeDtypeStruct((256, 24, 128), BF),
        in_specs=[S] * len(vectors) + [V] * len(arrays), out_specs=V,
        scratch_shapes=[
            pltpu.VMEM((ROWS, 256, 256), BF), pltpu.VMEM((256, ROWS, 128), BF), pltpu.VMEM((CB // 2, 224, 256), BF),
            pltpu.VMEM((256, 24, 128), F), pltpu.VMEM((24, 256, 128), BF), pltpu.VMEM((24, 256, 128), F),
            pltpu.VMEM((256, 768), BF),
        ],
        compiler_params=pltpu.CompilerParams(vmem_limit_bytes=48 * MIB),
    )(*vectors, *arrays)


def exchange(to_lower, to_upper, axis, wrap):
    size = lax.axis_size(axis)
    up = [(i, (i + 1) % size) for i in range(size if wrap else size - 1)]
    down = [(j, i) for i, j in up]
    return lax.ppermute(to_upper, axis, up), lax.ppermute(to_lower, axis, down)


def local(state, obs_values, obs_offsets, obs_cell, obs_count, w_in, dw_weight, dw_bias, norm_gain, norm_bias,
          w_up, up_bias, w_down, down_bias, layer_scale):
    row_base = (lax.axis_index("lat") * state.shape[1]).astype(jnp.int32).reshape(1)
    sums, up, down = observation_sums(obs_values, obs_offsets, obs_cell, obs_count, row_base, state)
    above, below = exchange(up, down, "lat", False)
    state_later, _ = lax.optimization_barrier((state, sums))
    rows, rims = state_rows(state_later)
    edge, left, right = edge_sums(sums, rims, above, below)
    from_left, from_right = exchange(left, right, "lon", True)
    dw_later, w_up_later, w_down_later, _ = lax.optimization_barrier((dw_weight, w_up, w_down, edge))
    toe, wi, w1, w2, b1 = prepare(dw_later, w_in, w_up_later, w_down_later, up_bias)
    return block(
        (sums, edge, above, below, rows, from_left, from_right, toe, wi, w1, b1, w2),
        (dw_bias, norm_gain, norm_bias, down_bias, layer_scale),
    )


def solution(mesh):
    return jax.shard_map(
        local,
        mesh=mesh,
        in_specs=(
            P(None, "lat", "lon"),
            P(None, ("lat", "lon")),
            P(None, ("lat", "lon")),
            P(("lat", "lon")),
            P(("lat", "lon")),
            P(),
            P(),
            P(),
            P(),
            P(),
            P(),
            P(),
            P(),
            P(),
            P(),
        ),
        out_specs=P(None, "lat", "lon"),
        check_vma=False,
    )
```

```python
import jax
import jax.numpy as jnp
from jax import lax
from jax.experimental import pallas as pl
from jax.experimental.pallas import tpu as pltpu
from jax.sharding import PartitionSpec as P

W = 4
SRC = 80
ROWS = 32
OBS_BLOCK = 512
GRID_ROWS = 384
CB = 16
RB = 4
BF = jnp.bfloat16
F = jnp.float32
MIB = 2**20
LAT_STATE = 9 * SRC
LAT_MSG = 9 * SRC + 3 * 256
LON_STATE = 2 * SRC
LON_MSG = 2 * SRC + 2 * 256

inverse_width = 1.0 / (2.0 * 1.5 * 1.5)


def lanes(rows):
    return lax.broadcasted_iota(jnp.int32, (rows, 128), 1)


def sums_kernel(count, row_base, vals_in, offs_in, cell_in, state_in, sums, up, down, vals, offs, cell, state, scaled, acc, sems):
    live_count = count[0]
    copies = [
        pltpu.make_async_copy(vals_in, vals, sems.at[0]),
        pltpu.make_async_copy(offs_in, offs, sems.at[1]),
        pltpu.make_async_copy(cell_in, cell, sems.at[2]),
        pltpu.make_async_copy(state_in.at[:, 0:8, :], state.at[:, 0:8, :], sems.at[3]),
        pltpu.make_async_copy(state_in.at[:, 16:24, :], state.at[:, 8:16, :], sems.at[4]),
    ]
    for copy in copies:
        copy.start()
    acc[...] = jnp.zeros(acc.shape, F)
    for copy in copies[:3]:
        copy.wait()

    def add_block(b, _):
        k0 = pl.multiple_of(b * OBS_BLOCK, OBS_BLOCK)
        ks = pl.ds(k0, OBS_BLOCK)
        where_cell = cell[:, ks]
        row = where_cell >> 7
        col = where_cell & 127
        slot = lax.broadcasted_iota(jnp.int32, (1, OBS_BLOCK), 1) + k0
        row = jnp.where(slot < live_count, row, -100)

        def weight(offset, place, centre, valid):
            apart = place - centre
            spread = offset - apart.astype(F) - 0.5
            inside = (jnp.abs(apart) <= W) & valid
            return jnp.where(inside, jnp.exp(-spread * spread * inverse_width), 0.0)

        place = lax.broadcasted_iota(jnp.int32, (ROWS, OBS_BLOCK), 0) - W
        on_grid = (place + row_base[0] >= 0) & (place + row_base[0] < GRID_ROWS)
        lat_weight = weight(offs[0:1, ks], place, row, on_grid)
        place = lax.broadcasted_iota(jnp.int32, (136, OBS_BLOCK), 0)
        first = weight(offs[1:2, ks], place, col, place < 128 + W)
        place = lax.broadcasted_iota(jnp.int32, (8, OBS_BLOCK), 0) - 8
        last = weight(offs[1:2, ks], place, col, place >= -W)
        lon_weight = jnp.concatenate([first, jnp.zeros((112, OBS_BLOCK), F), last], 0).astype(BF)
        ones = jnp.where(lax.broadcasted_iota(jnp.int32, (SRC - 64, OBS_BLOCK), 0) == 0, 1.0, 0.0)
        v = jnp.concatenate([vals[:, ks].astype(F), ones], 0)
        for p in range(ROWS):
            scaled[p * SRC:(p + 1) * SRC] = (v * lat_weight[p:p + 1]).astype(BF)
        for m in range(0, ROWS * SRC, 640):
            acc[m:m + 640] += lax.dot_general(
                scaled[m:m + 640], lon_weight, (((1,), (1,)), ((), ())), preferred_element_type=F)
        return 0

    lax.fori_loop(0, (live_count + OBS_BLOCK - 1) // OBS_BLOCK, add_block, 0)
    for copy in copies[3:]:
        copy.wait()
    for p in range(ROWS):
        sums[p] = acc[p * SRC:(p + 1) * SRC].astype(BF)
    for msg, first, state_tile, state_row in ((up, 0, 0, 0), (down, 24, 8, 5)):
        side = jnp.zeros((SRC, 128), F)
        for i in range(8):
            part = acc[(first + i) * SRC:(first + i + 1) * SRC]
            msg[i * SRC:(i + 1) * SRC] = part[:, :128].astype(BF)
            moved = pltpu.roll(part[:, 128:], i * 8 + 4, 1)
            side = jnp.where((lanes(SRC) >> 3) == i, moved, side)
        msg[8 * SRC:9 * SRC] = side.astype(BF)
        for c in range(0, 256, 16):
            x = jnp.swapaxes(state[c:c + 16, state_tile:state_tile + 8, :].astype(F), 0, 1).astype(BF)
            for j in range(3):
                msg[LAT_STATE + j * 256 + c:LAT_STATE + j * 256 + c + 16] = x[state_row + j]


def observation_sums(obs_values, obs_offsets, obs_cell, obs_count, row_base, state):
    S = pl.BlockSpec(memory_space=pltpu.SMEM)
    V = pl.BlockSpec(memory_space=pltpu.VMEM)
    shape = jax.ShapeDtypeStruct
    return pl.pallas_call(
        sums_kernel, name="observation_sums",
        out_shape=(shape((ROWS, SRC, 256), BF), shape((LAT_MSG, 128), BF), shape((LAT_MSG, 128), BF)),
        in_specs=[S, S] + [pl.BlockSpec(memory_space=pl.ANY)] * 4, out_specs=(V,) * 3,
        scratch_shapes=[
            pltpu.VMEM((64, 2048), BF), pltpu.VMEM((2, 2048), F), pltpu.VMEM((1, 2048), jnp.int32), pltpu.VMEM((256, 16, 128), BF),
            pltpu.VMEM((ROWS * SRC, OBS_BLOCK), BF), pltpu.VMEM((ROWS * SRC, 256), F), pltpu.SemaphoreType.DMA((5,)),
        ],
        compiler_params=pltpu.CompilerParams(vmem_limit_bytes=32 * MIB),
    )(obs_count, row_base, obs_values, obs_offsets, obs_cell.reshape(1, -1), state)


def pack(packed, p, main, side):
    lane = lanes(SRC)
    k, shift = p // 16, (p % 16) * 8 + 4
    here = (lane >> 3) == p % 16
    packed[0][k] = jnp.where(here, pltpu.roll(jnp.where(lane < 4, main, side), shift, 1), packed[0][k])
    packed[1][k] = jnp.where(here, pltpu.roll(jnp.where(lane >= 124, main, side), shift, 1), packed[1][k])


def rows_kernel(state, sums, rows, rims):
    def turn(i, _):
        c0 = pl.multiple_of(i * 16, 16)
        rows[:, pl.ds(c0, 16), :] = jnp.swapaxes(state[pl.ds(c0, 16)].astype(F), 0, 1).astype(BF)
        return 0

    lax.fori_loop(0, 16, turn, 0)
    for c in range(0, 256, 64):
        packed = [jnp.zeros((64, 128), F) for _ in range(2)]
        for r in range(24):
            p = r + W
            moved = pltpu.roll(rows[r, c:c + 64, :].astype(F), (p % 16) * 8 + 4, 1)
            packed[p // 16] = jnp.where((lanes(64) >> 3) == p % 16, moved, packed[p // 16])
        for k in range(2):
            rims[LON_STATE + k * 256 + c:LON_STATE + k * 256 + c + 64] = packed[k].astype(BF)
    packed = [[jnp.zeros((SRC, 128), F) for _ in range(2)] for _ in range(2)]
    for p in range(8, 24):
        pack(packed, p, sums[p, :, :128].astype(F), sums[p, :, 128:].astype(F))
    for k in range(2):
        rims[k * SRC:(k + 1) * SRC] = packed[0][k].astype(BF)
        rims[LON_MSG + k * SRC:LON_MSG + (k + 1) * SRC] = packed[1][k].astype(BF)


def state_rows(state, sums):
    shape = jax.ShapeDtypeStruct
    return pl.pallas_call(
        rows_kernel, name="state_rows", out_shape=(shape((24, 256, 128), BF), shape((LON_MSG + LON_STATE, 128), BF)),
        cost_estimate=pl.CostEstimate(flops=10**7, bytes_accessed=8 * 10**6, transcendentals=0),
        compiler_params=pltpu.CompilerParams(vmem_limit_bytes=16 * MIB),
    )(state, sums)


def edge_kernel(sums, rims, above, below, edge, left, right):
    lane = lanes(SRC)
    outer = (lane < 4) | (lane >= 124)
    packed = [[rims[first + k * SRC:first + (k + 1) * SRC].astype(F) for k in range(2)] for first in (0, LON_MSG)]
    for e in range(16):
        p = e if e < 8 else e + 16
        msg, i = (above, p) if p < 8 else (below, p - 24)
        moved = pltpu.roll(msg[8 * SRC:9 * SRC].astype(F), 124 - i * 8, 1)
        main = sums[p, :, :128].astype(F) + msg[i * SRC:(i + 1) * SRC].astype(F)
        side = sums[p, :, 128:].astype(F) + jnp.where(outer, moved, 0.0)
        edge[e] = main.astype(BF)
        pack(packed, p, main, side)
    for k in range(2):
        left[k * SRC:(k + 1) * SRC] = packed[0][k].astype(BF)
        right[k * SRC:(k + 1) * SRC] = packed[1][k].astype(BF)
    for c in range(0, 256, 64):
        for k, msg, first in ((0, above, 1), (1, below, 28)):
            at = LON_STATE + k * 256 + c
            out = rims[at:at + 64].astype(F)
            for j in range(3):
                p = first + j
                x = msg[LAT_STATE + j * 256 + c:LAT_STATE + j * 256 + c + 64].astype(F)
                out = jnp.where((lanes(64) >> 3) == p % 16, pltpu.roll(x, (p % 16) * 8 + 4, 1), out)
            left[at:at + 64] = out.astype(BF)
            right[at:at + 64] = out.astype(BF)


def edge_sums(sums, rims, above, below):
    shape = jax.ShapeDtypeStruct
    return pl.pallas_call(
        edge_kernel, name="edge_sums",
        out_shape=(shape((16, SRC, 128), BF), shape((LON_MSG, 128), BF), shape((LON_MSG, 128), BF)),
        compiler_params=pltpu.CompilerParams(vmem_limit_bytes=16 * MIB),
    )(sums, rims, above, below)


def prepare_kernel(taps, w_in, w_up, w_down, b1, toe, wi, w1, w2, b1c, smat, padded, base):
    smat[...] = shift_matrix()
    padded[...] = jnp.zeros(padded.shape, F)
    padded[0:65] = w_in[...].astype(F)
    wi[...] = padded[...].T.astype(BF)
    w1[...] = w_up[...].T
    w2[...] = w_down[...].T
    b1c[...] = b1[...].T
    base[...] = jnp.zeros(base.shape, F)
    for v in range(7):
        for u in range(7):
            base[32 * v + 1 + u:32 * v + 2 + u] = taps[u, v:v + 1]
    base[...] = base[...].T

    def step(i, _):
        rows = base[pl.ds(pl.multiple_of(i * 8, 8), 8), :]
        for k in range(8):
            parts = []
            for ln in range(2):
                b = jnp.broadcast_to(rows[k:k + 1, ln * 128:(ln + 1) * 128], (24, 128))
                parts.append(pltpu.roll(b, 0, 1, stride=1, stride_axis=0))
            y = jnp.concatenate(parts, 1).astype(BF)
            toe[i * 4 + k // 2, (k % 2) * 24:(k % 2) * 24 + 24, :] = y[:, :224]
        return 0

    lax.fori_loop(0, 32, step, 0)


def prepare(dw_weight, w_in, w_up, w_down, up_bias):
    shape = jax.ShapeDtypeStruct
    return pl.pallas_call(
        prepare_kernel, name="prepare",
        out_shape=(shape((128, 48, 224), BF), shape((256, SRC), BF), shape((1024, 256), BF), shape((256, 1024), BF), shape((128, 8), F), shape((256, 768), BF)),
        scratch_shapes=[pltpu.VMEM((SRC, 256), F), pltpu.VMEM((256, 256), F)],
        cost_estimate=pl.CostEstimate(flops=10**7, bytes_accessed=8 * 10**6, transcendentals=0),
        compiler_params=pltpu.CompilerParams(vmem_limit_bytes=16 * MIB),
    )(jnp.transpose(dw_weight, (1, 2, 0)), w_in, w_up, w_down, up_bias.reshape(8, 128))


def shift_matrix():
    lane = lax.broadcasted_iota(jnp.int32, (256, 768), 0)
    out = lax.broadcasted_iota(jnp.int32, (256, 768), 1)
    j = lane & 7
    col = jnp.where(lane < 128, lane, jnp.where(j < 4, j - 4, j + 124))
    k = out // 128
    d = jnp.where(k < 3, k - 3, k - 2)
    return jnp.where(col == out % 128 + d, 1.0, 0.0).astype(BF)


def block_kernel(dwb, gain, nbias, db, ls, sums, edge, above, below, rows, left, right, from_left, from_right,
                 toe, wi, w1, b1, w2, smat, out, mixed, native, sides, inward, mext, xs, filt, xbuf, obuf):
    lane = lanes(SRC)
    outer = (lane < 4) | (lane >= 124)
    first = (lane & 7) < 4
    parts = []
    for k in range(2):
        at = slice(k * SRC, (k + 1) * SRC)
        a, b = from_left[at].astype(F), from_right[at].astype(F)
        inward[at] = jnp.where(first, b, a)
        parts.append(jnp.where(first, left[at].astype(F) + a, right[at].astype(F) + b))
    both = jnp.dot(wi[...], jnp.concatenate(parts, 1).astype(BF), preferred_element_type=F)
    for k in range(2):
        at = slice(LON_STATE + k * 256, LON_STATE + k * 256 + 256)
        rim = jnp.where((lanes(256) & 7) < 4, from_left[at].astype(F), from_right[at].astype(F))
        sides[:, k * 128:(k + 1) * 128] = (both[:, k * 128:(k + 1) * 128] + rim).astype(BF).astype(F)

    def encode(*cases):
        parts = []
        for p, main, _ in cases:
            at = pl.ds(pl.multiple_of(p // 16 * SRC, SRC), SRC)
            moved = pltpu.roll(inward[at], (124 - (p % 16) * 8) % 128, 1)
            parts.append((main.astype(F) + jnp.where(outer, moved, 0.0)).astype(BF))
        both = jnp.dot(wi[...], jnp.concatenate(parts, 1), preferred_element_type=F)
        for n, (p, _, state) in enumerate(cases):
            mixed[p] = (both[:, n * 128:(n + 1) * 128] + state.astype(F)).astype(BF)

    mixed[0] = jnp.zeros((256, 128), BF)
    mixed[31] = jnp.zeros((256, 128), BF)
    for j in range(3):
        at = slice(LAT_STATE + j * 256, LAT_STATE + j * 256 + 256)
        encode((1 + j, edge[1 + j], above[at]), (28 + j, edge[12 + j], below[at]))

    def edge_row(j, _):
        encode((4 + j, edge[4 + j], rows[j]), (24 + j, edge[8 + j], rows[20 + j]))
        return 0

    def inner_row(j, _):
        encode((8 + j, sums[8 + j, :, :128], rows[4 + j]), (16 + j, sums[16 + j, :, :128], rows[12 + j]))
        return 0

    lax.fori_loop(0, 4, edge_row, 0)
    lax.fori_loop(0, 8, inner_row, 0)
    slot = (lanes(16) >> 3) == lax.broadcasted_iota(jnp.int32, (16, 128), 0)

    def filt_step(i, carry):
        pivot, s1, s2 = carry
        c0 = pl.multiple_of(i * CB, CB)
        turned = jnp.swapaxes(mixed[:, pl.ds(c0, CB), :].astype(F), 0, 1).astype(BF)
        native[pl.ds(c0, CB)] = turned
        side = sides[pl.ds(c0, CB)]
        for c in range(CB):
            mext[c * 32:(c + 1) * 32, :128] = turned[c]
            for k in range(2):
                spread = jnp.broadcast_to(side[c:c + 1, k * 128:(k + 1) * 128], (16, 128))
                mext[c * 32 + k * 16:c * 32 + k * 16 + 16, 128:] = jnp.where(slot, spread, 0.0).astype(BF)
            xs[c // 2, 96:128, (c % 2) * 128:(c % 2) * 128 + 128] = turned[c]
        for j in range(3):
            z = jnp.dot(mext[...], smat[:, j * 256:(j + 1) * 256], preferred_element_type=F).astype(BF)
            for half in range(2):
                k = 2 * j + half
                v = k if k < 3 else k + 1
                zz = z[:, half * 128:(half + 1) * 128]
                for c in range(CB):
                    xs[c // 2, v * 32:(v + 1) * 32, (c % 2) * 128:(c % 2) * 128 + 128] = zz[c * 32:(c + 1) * 32]
        for k in range(CB // 2):
            o = jnp.dot(toe[i * (CB // 2) + k], xs[k], preferred_element_type=F)
            for c, y in ((c0 + 2 * k, o[:24, :128]), (c0 + 2 * k + 1, o[24:, 128:])):
                y = y + dwb[c]
                if k == 0:
                    pivot = jnp.where(c == 0, y, pivot)
                y = y - pivot
                filt[c] = y
                s1 = s1 + y
                s2 = s2 + y * y
        return pivot, s1, s2

    zero = jnp.zeros((24, 128), F)
    _, s1, s2 = lax.fori_loop(0, 256 // CB, filt_step, (zero, zero, zero))
    mean = s1 * (1.0 / 256)
    rstd = lax.rsqrt(jnp.maximum(s2 * (1.0 / 256) - mean * mean, 0.0) + 1e-6)

    def norm_step(i, _):
        c0 = pl.multiple_of(i * 16, 16)
        ys = [((filt[c0 + k] - mean) * rstd) * gain[c0 + k] + nbias[c0 + k] for k in range(16)]
        xbuf[:, pl.ds(c0, 16), :] = jnp.swapaxes(jnp.stack(ys, 0), 0, 1).astype(BF)
        return 0

    lax.fori_loop(0, 16, norm_step, 0)

    def mlp_step(i, _):
        x = jnp.concatenate([xbuf[i * RB + k] for k in range(RB)], 1)
        h = jnp.dot(w1[...], x, preferred_element_type=F)
        gs = []
        for k in range(8):
            hk = h[k * 128:(k + 1) * 128] + b1[:, k:k + 1]
            gs.append(((0.5 * hk) * (1.0 + lax.erf(hk * 0.7071067811865476))).astype(BF))
        o = jnp.dot(w2[...], jnp.concatenate(gs, 0), preferred_element_type=F)
        for k in range(RB):
            obuf[i * RB + k] = o[:, k * 128:(k + 1) * 128]
        return 0

    lax.fori_loop(0, 24 // RB, mlp_step, 0)

    def out_step(i, _):
        c0 = pl.multiple_of(i * 16, 16)
        o = jnp.swapaxes(obuf[:, pl.ds(c0, 16), :], 0, 1)
        m = native[pl.ds(c0, 16)].astype(F)
        for k in range(16):
            out[c0 + k] = (m[k, 4:28] + (o[k] + db[c0 + k]) * ls[c0 + k]).astype(BF)
        return 0

    lax.fori_loop(0, 16, out_step, 0)


def block(arrays, vectors):
    S = pl.BlockSpec(memory_space=pltpu.SMEM)
    V = pl.BlockSpec(memory_space=pltpu.VMEM)
    return pl.pallas_call(
        block_kernel, name="block", out_shape=jax.ShapeDtypeStruct((256, 24, 128), BF),
        in_specs=[S] * len(vectors) + [V] * len(arrays), out_specs=V,
        scratch_shapes=[
            pltpu.VMEM((ROWS, 256, 128), BF), pltpu.VMEM((256, ROWS, 128), BF), pltpu.VMEM((256, 256), F), pltpu.VMEM((2 * SRC, 128), F),
            pltpu.VMEM((CB * 32, 256), BF), pltpu.VMEM((CB // 2, 224, 256), BF),
            pltpu.VMEM((256, 24, 128), F), pltpu.VMEM((24, 256, 128), BF), pltpu.VMEM((24, 256, 128), F),
        ],
        compiler_params=pltpu.CompilerParams(vmem_limit_bytes=30 * MIB),
    )(*vectors, *arrays)


def exchange(to_lower, to_upper, axis, wrap):
    size = lax.axis_size(axis)
    up = [(i, (i + 1) % size) for i in range(size if wrap else size - 1)]
    down = [(j, i) for i, j in up]
    return lax.ppermute(to_upper, axis, up), lax.ppermute(to_lower, axis, down)


def local(state, obs_values, obs_offsets, obs_cell, obs_count, w_in, dw_weight, dw_bias, norm_gain, norm_bias,
          w_up, up_bias, w_down, down_bias, layer_scale):
    row_base = (lax.axis_index("lat") * state.shape[1]).astype(jnp.int32).reshape(1)
    sums, up, down = observation_sums(obs_values, obs_offsets, obs_cell, obs_count, row_base, state)
    above, below = exchange(up, down, "lat", False)
    rows, rims = state_rows(state, sums)
    edge, left, right = edge_sums(sums, rims, above, below)
    from_left, from_right = exchange(left, right, "lon", True)
    dw_later, w_up_later, w_down_later, _ = lax.optimization_barrier((dw_weight, w_up, w_down, edge))
    toe, wi, w1, w2, b1, smat = prepare(dw_later, w_in, w_up_later, w_down_later, up_bias)
    return block(
        (sums, edge, above, below, rows, left, right, from_left, from_right, toe, wi, w1, b1, w2, smat),
        (dw_bias, norm_gain, norm_bias, down_bias, layer_scale),
    )


def solution(mesh):
    return jax.shard_map(
        local,
        mesh=mesh,
        in_specs=(
            P(None, "lat", "lon"),
            P(None, ("lat", "lon")),
            P(None, ("lat", "lon")),
            P(("lat", "lon")),
            P(("lat", "lon")),
            P(),
            P(),
            P(),
            P(),
            P(),
            P(),
            P(),
            P(),
            P(),
            P(),
        ),
        out_specs=P(None, "lat", "lon"),
        check_vma=False,
    )
```

```python
import jax
import jax.numpy as jnp
from jax import lax
from jax.experimental import pallas as pl
from jax.experimental.pallas import tpu as pltpu
from jax.sharding import PartitionSpec as P

W = 4
SRC = 80
ROWS = 32
OBS_BLOCK = 512
GRID_ROWS = 384
CB = 16
RB = 4
BF = jnp.bfloat16
F = jnp.float32
MIB = 2**20
LAT_STATE = 9 * SRC
LAT_MSG = 9 * SRC + 3 * 256
LON_STATE = 2 * SRC
LON_MSG = 2 * SRC + 256
RIMS = 2 * SRC + 2 * 256

inverse_width = 1.0 / (2.0 * 1.5 * 1.5)


def lanes(rows):
    return lax.broadcasted_iota(jnp.int32, (rows, 128), 1)


def sums_kernel(count, row_base, vals_in, offs_in, cell_in, state_in, sums, up, down, vals, offs, cell, state, scaled, acc, sems):
    live_count = count[0]
    copies = [
        pltpu.make_async_copy(vals_in, vals, sems.at[0]),
        pltpu.make_async_copy(offs_in, offs, sems.at[1]),
        pltpu.make_async_copy(cell_in, cell, sems.at[2]),
        pltpu.make_async_copy(state_in.at[:, 0:8, :], state.at[:, 0:8, :], sems.at[3]),
        pltpu.make_async_copy(state_in.at[:, 16:24, :], state.at[:, 8:16, :], sems.at[4]),
    ]
    for copy in copies:
        copy.start()
    acc[...] = jnp.zeros(acc.shape, F)
    for copy in copies[:3]:
        copy.wait()

    def add_block(b, _):
        k0 = pl.multiple_of(b * OBS_BLOCK, OBS_BLOCK)
        ks = pl.ds(k0, OBS_BLOCK)
        where_cell = cell[:, ks]
        row = where_cell >> 7
        col = where_cell & 127
        slot = lax.broadcasted_iota(jnp.int32, (1, OBS_BLOCK), 1) + k0
        row = jnp.where(slot < live_count, row, -100)

        def weight(offset, place, centre, valid):
            apart = place - centre
            spread = offset - apart.astype(F) - 0.5
            inside = (jnp.abs(apart) <= W) & valid
            return jnp.where(inside, jnp.exp(-spread * spread * inverse_width), 0.0)

        place = lax.broadcasted_iota(jnp.int32, (ROWS, OBS_BLOCK), 0) - W
        on_grid = (place + row_base[0] >= 0) & (place + row_base[0] < GRID_ROWS)
        lat_weight = weight(offs[0:1, ks], place, row, on_grid)
        place = lax.broadcasted_iota(jnp.int32, (136, OBS_BLOCK), 0)
        first = weight(offs[1:2, ks], place, col, place < 128 + W)
        place = lax.broadcasted_iota(jnp.int32, (8, OBS_BLOCK), 0) - 8
        last = weight(offs[1:2, ks], place, col, place >= -W)
        lon_weight = jnp.concatenate([first, jnp.zeros((112, OBS_BLOCK), F), last], 0).astype(BF)
        ones = jnp.where(lax.broadcasted_iota(jnp.int32, (SRC - 64, OBS_BLOCK), 0) == 0, 1.0, 0.0)
        v = jnp.concatenate([vals[:, ks].astype(F), ones], 0)
        for p in range(ROWS):
            scaled[p * SRC:(p + 1) * SRC] = (v * lat_weight[p:p + 1]).astype(BF)
        for m in range(0, ROWS * SRC, 640):
            acc[m:m + 640] += lax.dot_general(
                scaled[m:m + 640], lon_weight, (((1,), (1,)), ((), ())), preferred_element_type=F)
        return 0

    lax.fori_loop(0, (live_count + OBS_BLOCK - 1) // OBS_BLOCK, add_block, 0)
    for copy in copies[3:]:
        copy.wait()
    for p in range(ROWS):
        sums[p] = acc[p * SRC:(p + 1) * SRC].astype(BF)
    for msg, first, state_tile, state_row in ((up, 0, 0, 0), (down, 24, 8, 5)):
        side = jnp.zeros((SRC, 128), F)
        for i in range(8):
            part = acc[(first + i) * SRC:(first + i + 1) * SRC]
            msg[i * SRC:(i + 1) * SRC] = part[:, :128].astype(BF)
            moved = pltpu.roll(part[:, 128:], i * 8 + 4, 1)
            side = jnp.where((lanes(SRC) >> 3) == i, moved, side)
        msg[8 * SRC:9 * SRC] = side.astype(BF)
        for c in range(0, 256, 16):
            x = jnp.swapaxes(state[c:c + 16, state_tile:state_tile + 8, :].astype(F), 0, 1).astype(BF)
            for j in range(3):
                msg[LAT_STATE + j * 256 + c:LAT_STATE + j * 256 + c + 16] = x[state_row + j]


def observation_sums(obs_values, obs_offsets, obs_cell, obs_count, row_base, state):
    S = pl.BlockSpec(memory_space=pltpu.SMEM)
    V = pl.BlockSpec(memory_space=pltpu.VMEM)
    shape = jax.ShapeDtypeStruct
    return pl.pallas_call(
        sums_kernel, name="observation_sums",
        out_shape=(shape((ROWS, SRC, 256), BF), shape((LAT_MSG, 128), BF), shape((LAT_MSG, 128), BF)),
        in_specs=[S, S] + [pl.BlockSpec(memory_space=pl.ANY)] * 4, out_specs=(V,) * 3,
        scratch_shapes=[
            pltpu.VMEM((64, 2048), BF), pltpu.VMEM((2, 2048), F), pltpu.VMEM((1, 2048), jnp.int32), pltpu.VMEM((256, 16, 128), BF),
            pltpu.VMEM((ROWS * SRC, OBS_BLOCK), BF), pltpu.VMEM((ROWS * SRC, 256), F), pltpu.SemaphoreType.DMA((5,)),
        ],
        compiler_params=pltpu.CompilerParams(vmem_limit_bytes=56 * MIB),
    )(obs_count, row_base, obs_values, obs_offsets, obs_cell.reshape(1, -1), state)


def place(p):
    return 15 - p % 16


def pack(packed, p, main, side):
    lane = lanes(SRC)
    k, shift = p // 16, place(p) * 8 + 4
    here = (lane >> 3) == place(p)
    packed[0][k] = jnp.where(here, pltpu.roll(jnp.where(lane < 4, main, side), shift, 1), packed[0][k])
    packed[1][k] = jnp.where(here, pltpu.roll(jnp.where(lane >= 124, main, side), shift, 1), packed[1][k])


def rows_kernel(state, sums, rows, rims):
    def turn(i, _):
        c0 = pl.multiple_of(i * 16, 16)
        rows[:, pl.ds(c0, 16), :] = jnp.swapaxes(state[pl.ds(c0, 16)].astype(F), 0, 1).astype(BF)
        return 0

    lax.fori_loop(0, 16, turn, 0)
    for c in range(0, 256, 64):
        packed = [jnp.zeros((64, 128), F) for _ in range(2)]
        for r in range(24):
            p = r + W
            moved = pltpu.roll(rows[r, c:c + 64, :].astype(F), place(p) * 8 + 4, 1)
            packed[p // 16] = jnp.where((lanes(64) >> 3) == place(p), moved, packed[p // 16])
        for k in range(2):
            rims[LON_STATE + k * 256 + c:LON_STATE + k * 256 + c + 64] = packed[k].astype(BF)
    packed = [[jnp.zeros((SRC, 128), F) for _ in range(2)] for _ in range(2)]
    for p in range(8, 24):
        pack(packed, p, sums[p, :, :128].astype(F), sums[p, :, 128:].astype(F))
    for k in range(2):
        rims[k * SRC:(k + 1) * SRC] = packed[0][k].astype(BF)
        rims[RIMS + k * SRC:RIMS + (k + 1) * SRC] = packed[1][k].astype(BF)


def state_rows(state, sums):
    shape = jax.ShapeDtypeStruct
    return pl.pallas_call(
        rows_kernel, name="state_rows", out_shape=(shape((24, 256, 128), BF), shape((RIMS + LON_STATE, 128), BF)),
        cost_estimate=pl.CostEstimate(flops=10**7, bytes_accessed=8 * 10**6, transcendentals=0),
        compiler_params=pltpu.CompilerParams(vmem_limit_bytes=16 * MIB),
    )(state, sums)


def edge_kernel(sums, rims, above, below, edge, left, right):
    lane = lanes(SRC)
    outer = (lane < 4) | (lane >= 124)
    packed = [[rims[first + k * SRC:first + (k + 1) * SRC].astype(F) for k in range(2)] for first in (0, RIMS)]
    for e in range(16):
        p = e if e < 8 else e + 16
        msg, i = (above, p) if p < 8 else (below, p - 24)
        moved = pltpu.roll(msg[8 * SRC:9 * SRC].astype(F), 124 - i * 8, 1)
        main = sums[p, :, :128].astype(F) + msg[i * SRC:(i + 1) * SRC].astype(F)
        side = sums[p, :, 128:].astype(F) + jnp.where(outer, moved, 0.0)
        edge[e] = main.astype(BF)
        pack(packed, p, main, side)
    for k in range(2):
        left[k * SRC:(k + 1) * SRC] = packed[0][k].astype(BF)
        right[k * SRC:(k + 1) * SRC] = packed[1][k].astype(BF)
    early = (lanes(64) & 7) < 4
    for c in range(0, 256, 64):
        halves = []
        for k, msg, first in ((0, above, 1), (1, below, 28)):
            at = LON_STATE + k * 256 + c
            out = rims[at:at + 64].astype(F)
            for j in range(3):
                p = first + j
                x = msg[LAT_STATE + j * 256 + c:LAT_STATE + j * 256 + c + 64].astype(F)
                out = jnp.where((lanes(64) >> 3) == place(p), pltpu.roll(x, place(p) * 8 + 4, 1), out)
            halves.append(out)
        at = slice(LON_STATE + c, LON_STATE + c + 64)
        left[at] = jnp.where(early, pltpu.roll(halves[1], 124, 1), halves[0]).astype(BF)
        right[at] = jnp.where(early, halves[0], pltpu.roll(halves[1], 4, 1)).astype(BF)


def edge_sums(sums, rims, above, below):
    shape = jax.ShapeDtypeStruct
    return pl.pallas_call(
        edge_kernel, name="edge_sums",
        out_shape=(shape((16, SRC, 128), BF), shape((LON_MSG, 128), BF), shape((LON_MSG, 128), BF)),
        compiler_params=pltpu.CompilerParams(vmem_limit_bytes=16 * MIB),
    )(sums, rims, above, below)


def prepare_kernel(taps, w_in, w_up, w_down, b1, toe, wi, w1, w2, b1c, smat, padded, base):
    smat[...] = shift_matrix()
    padded[...] = jnp.zeros(padded.shape, F)
    padded[0:65] = w_in[...].astype(F)
    wi[...] = padded[...].T.astype(BF)
    w1[...] = w_up[...].T
    w2[...] = w_down[...].T
    b1c[...] = b1[...].T
    base[...] = jnp.zeros(base.shape, F)
    for v in range(7):
        for u in range(7):
            base[32 * v + 1 + u:32 * v + 2 + u] = taps[u, v:v + 1]
    base[...] = base[...].T

    def step(i, _):
        rows = base[pl.ds(pl.multiple_of(i * 8, 8), 8), :]
        for k in range(8):
            parts = []
            for ln in range(2):
                b = jnp.broadcast_to(rows[k:k + 1, ln * 128:(ln + 1) * 128], (24, 128))
                parts.append(pltpu.roll(b, 0, 1, stride=1, stride_axis=0))
            y = jnp.concatenate(parts, 1).astype(BF)
            toe[i * 4 + k // 2, (k % 2) * 24:(k % 2) * 24 + 24, :] = y[:, :224]
        return 0

    lax.fori_loop(0, 32, step, 0)


def prepare(dw_weight, w_in, w_up, w_down, up_bias):
    shape = jax.ShapeDtypeStruct
    return pl.pallas_call(
        prepare_kernel, name="prepare",
        out_shape=(shape((128, 48, 224), BF), shape((256, SRC), BF), shape((1024, 256), BF), shape((256, 1024), BF), shape((128, 8), F), shape((256, 768), BF)),
        scratch_shapes=[pltpu.VMEM((SRC, 256), F), pltpu.VMEM((256, 256), F)],
        cost_estimate=pl.CostEstimate(flops=10**7, bytes_accessed=8 * 10**6, transcendentals=0),
        compiler_params=pltpu.CompilerParams(vmem_limit_bytes=16 * MIB),
    )(jnp.transpose(dw_weight, (1, 2, 0)), w_in, w_up, w_down, up_bias.reshape(8, 128))


def shift_matrix():
    lane = lax.broadcasted_iota(jnp.int32, (256, 768), 0)
    out = lax.broadcasted_iota(jnp.int32, (256, 768), 1)
    j = lane & 7
    col = jnp.where(lane < 128, lane, jnp.where(j < 4, j - 4, j + 124))
    k = out // 128
    d = jnp.where(k < 3, k - 3, k - 2)
    return jnp.where(col == out % 128 + d, 1.0, 0.0).astype(BF)


def encode_kernel(sums, edge, above, below, rows, wi, native, mixed):
    def encode(*cases):
        both = jnp.dot(wi[...], jnp.concatenate([main for _, main, _ in cases], 1), preferred_element_type=F)
        for n, (p, _, state) in enumerate(cases):
            mixed[p] = (both[:, n * 128:(n + 1) * 128] + state.astype(F)).astype(BF)

    mixed[0] = jnp.zeros((256, 128), BF)
    mixed[31] = jnp.zeros((256, 128), BF)
    for j in range(3):
        at = slice(LAT_STATE + j * 256, LAT_STATE + j * 256 + 256)
        encode((1 + j, edge[1 + j], above[at]), (28 + j, edge[12 + j], below[at]))

    def edge_row(j, _):
        encode((4 + j, edge[4 + j], rows[j]), (24 + j, edge[8 + j], rows[20 + j]))
        return 0

    def inner_row(j, _):
        encode((8 + j, sums[8 + j, :, :128], rows[4 + j]), (16 + j, sums[16 + j, :, :128], rows[12 + j]))
        return 0

    lax.fori_loop(0, 4, edge_row, 0)
    lax.fori_loop(0, 8, inner_row, 0)

    def turn(i, _):
        c0 = pl.multiple_of(i * CB, CB)
        native[pl.ds(c0, CB)] = jnp.swapaxes(mixed[:, pl.ds(c0, CB), :].astype(F), 0, 1).astype(BF)
        return 0

    lax.fori_loop(0, 256 // CB, turn, 0)


def encode(*arrays):
    return pl.pallas_call(
        encode_kernel, name="encode", out_shape=jax.ShapeDtypeStruct((256, ROWS, 128), BF),
        scratch_shapes=[pltpu.VMEM((ROWS, 256, 128), BF)],
        cost_estimate=pl.CostEstimate(flops=10**8, bytes_accessed=8 * 10**6, transcendentals=0),
        compiler_params=pltpu.CompilerParams(vmem_limit_bytes=20 * MIB),
    )(*arrays)


def block_kernel(dwb, gain, nbias, db, ls, partial, left, right, from_left, from_right,
                 toe, wi, w1, b1, w2, smat, out, native, sides, inward, mext, xs, filt, xbuf, obuf, result, sems):
    first = (lanes(SRC) & 7) < 4
    parts = []
    for k in range(2):
        at = slice(k * SRC, (k + 1) * SRC)
        a, b = from_left[at].astype(F), from_right[at].astype(F)
        parts.append(jnp.where(first, left[at].astype(F) + a, right[at].astype(F) + b))
        parts.append(jnp.where(first, b, a))
    both = jnp.dot(wi[...], jnp.concatenate(parts, 1).astype(BF), preferred_element_type=F)
    first = (lanes(256) & 7) < 4
    a, b = from_left[LON_STATE:LON_STATE + 256].astype(F), from_right[LON_STATE:LON_STATE + 256].astype(F)
    rims = (jnp.where(first, a, b), jnp.where(first, pltpu.roll(a, 124, 1), pltpu.roll(b, 4, 1)))
    for k in range(2):
        sides[:, k * 128:(k + 1) * 128] = (both[:, 2 * k * 128:(2 * k + 1) * 128] + rims[k]).astype(BF).astype(F)
        inward[:, k * 128:(k + 1) * 128] = both[:, (2 * k + 1) * 128:(2 * k + 2) * 128]
    slot = (lanes(16) >> 3) == 15 - lax.broadcasted_iota(jnp.int32, (16, 128), 0)
    outer = (lanes(16) < 4) | (lanes(16) >= 124)

    def filt_step(i, carry):
        pivot, s1, s2 = carry
        c0 = pl.multiple_of(i * CB, CB)
        side, more = sides[pl.ds(c0, CB)], inward[pl.ds(c0, CB)]
        for c in range(CB):
            for k in range(2):
                at = slice(c * 32 + k * 16, c * 32 + k * 16 + 16)
                ks = slice(k * 128, (k + 1) * 128)
                spread = jnp.broadcast_to(side[c:c + 1, ks], (16, 128))
                mext[at, 128:] = jnp.where(slot, spread, 0.0).astype(BF)
                moved = pltpu.roll(jnp.broadcast_to(more[c:c + 1, ks], (16, 128)), 4, 1, stride=8, stride_axis=0)
                main = (partial[c0 + c, k * 16:k * 16 + 16].astype(F) + jnp.where(outer, moved, 0.0)).astype(BF)
                mext[at, :128] = main
                native[c0 + c, k * 16:k * 16 + 16] = main
                xs[c // 2, 96 + k * 16:112 + k * 16, (c % 2) * 128:(c % 2) * 128 + 128] = main
        for j in range(3):
            z = jnp.dot(mext[...], smat[:, j * 256:(j + 1) * 256], preferred_element_type=F).astype(BF)
            for half in range(2):
                k = 2 * j + half
                v = k if k < 3 else k + 1
                zz = z[:, half * 128:(half + 1) * 128]
                for c in range(CB):
                    xs[c // 2, v * 32:(v + 1) * 32, (c % 2) * 128:(c % 2) * 128 + 128] = zz[c * 32:(c + 1) * 32]
        for k in range(CB // 2):
            o = jnp.dot(toe[i * (CB // 2) + k], xs[k], preferred_element_type=F)
            for c, y in ((c0 + 2 * k, o[:24, :128]), (c0 + 2 * k + 1, o[24:, 128:])):
                y = y + dwb[c]
                if k == 0:
                    pivot = jnp.where(c == 0, y, pivot)
                y = y - pivot
                filt[c] = y
                s1 = s1 + y
                s2 = s2 + y * y
        return pivot, s1, s2

    zero = jnp.zeros((24, 128), F)
    _, s1, s2 = lax.fori_loop(0, 256 // CB, filt_step, (zero, zero, zero))
    mean = s1 * (1.0 / 256)
    rstd = lax.rsqrt(jnp.maximum(s2 * (1.0 / 256) - mean * mean, 0.0) + 1e-6)

    def norm_step(i, _):
        c0 = pl.multiple_of(i * 16, 16)
        ys = [((filt[c0 + k] - mean) * rstd) * gain[c0 + k] + nbias[c0 + k] for k in range(16)]
        xbuf[:, pl.ds(c0, 16), :] = jnp.swapaxes(jnp.stack(ys, 0), 0, 1).astype(BF)
        return 0

    lax.fori_loop(0, 16, norm_step, 0)

    def mlp_step(i, _):
        x = jnp.concatenate([xbuf[i * RB + k] for k in range(RB)], 1)
        h = jnp.dot(w1[...], x, preferred_element_type=F)
        gs = []
        for k in range(8):
            hk = h[k * 128:(k + 1) * 128] + b1[:, k:k + 1]
            gs.append(((0.5 * hk) * (1.0 + lax.erf(hk * 0.7071067811865476))).astype(BF))
        o = jnp.dot(w2[...], jnp.concatenate(gs, 0), preferred_element_type=F)
        for k in range(RB):
            obuf[i * RB + k] = o[:, k * 128:(k + 1) * 128]
        return 0

    lax.fori_loop(0, 24 // RB, mlp_step, 0)

    def out_step(i, _):
        c0 = pl.multiple_of(i * 16, 16)
        o = jnp.swapaxes(obuf[:, pl.ds(c0, 16), :], 0, 1)
        m = native[pl.ds(c0, 16)].astype(F)
        for k in range(16):
            result[c0 + k] = (m[k, 4:28] + (o[k] + db[c0 + k]) * ls[c0 + k]).astype(BF)
        return 0

    copies = []
    for n in range(4):
        lax.fori_loop(4 * n, 4 * n + 4, out_step, 0)
        at = slice(64 * n, 64 * n + 64)
        copies.append(pltpu.make_async_copy(result.at[at], out.at[at], sems.at[n]))
        copies[-1].start()
    for copy in copies:
        copy.wait()


def block(arrays, vectors):
    S = pl.BlockSpec(memory_space=pltpu.SMEM)
    V = pl.BlockSpec(memory_space=pltpu.VMEM)
    return pl.pallas_call(
        block_kernel, name="block", out_shape=jax.ShapeDtypeStruct((256, 24, 128), BF),
        in_specs=[S] * len(vectors) + [V] * len(arrays), out_specs=pl.BlockSpec(memory_space=pl.ANY),
        scratch_shapes=[
            pltpu.VMEM((256, ROWS, 128), BF), pltpu.VMEM((256, 256), F), pltpu.VMEM((256, 256), F),
            pltpu.VMEM((CB * 32, 256), BF), pltpu.VMEM((CB // 2, 224, 256), BF),
            pltpu.VMEM((256, 24, 128), F), pltpu.VMEM((24, 256, 128), BF), pltpu.VMEM((24, 256, 128), F),
            pltpu.VMEM((256, 24, 128), BF), pltpu.SemaphoreType.DMA((4,)),
        ],
        compiler_params=pltpu.CompilerParams(vmem_limit_bytes=30 * MIB),
    )(*vectors, *arrays)


def exchange(to_lower, to_upper, axis, wrap):
    size = lax.axis_size(axis)
    up = [(i, (i + 1) % size) for i in range(size if wrap else size - 1)]
    down = [(j, i) for i, j in up]
    return lax.ppermute(to_upper, axis, up), lax.ppermute(to_lower, axis, down)


def local(state, obs_values, obs_offsets, obs_cell, obs_count, w_in, dw_weight, dw_bias, norm_gain, norm_bias,
          w_up, up_bias, w_down, down_bias, layer_scale):
    row_base = (lax.axis_index("lat") * state.shape[1]).astype(jnp.int32).reshape(1)
    sums, up, down = observation_sums(obs_values, obs_offsets, obs_cell, obs_count, row_base, state)
    above, below = exchange(up, down, "lat", False)
    rows, rims = state_rows(state, sums)
    dw_later, w_up_later, w_down_later, _ = lax.optimization_barrier((dw_weight, w_up, w_down, rows))
    weights = prepare(dw_later, w_in, w_up_later, w_down_later, up_bias)
    rims, (toe, wi, w1, w2, b1, smat) = lax.optimization_barrier((rims, weights))
    edge, left, right = edge_sums(sums, rims, above, below)
    from_left, from_right = exchange(left, right, "lon", True)
    partial = encode(sums, edge, above, below, rows, wi)
    return block(
        (partial, left, right, from_left, from_right, toe, wi, w1, b1, w2, smat),
        (dw_bias, norm_gain, norm_bias, down_bias, layer_scale),
    )


def solution(mesh):
    return jax.shard_map(
        local,
        mesh=mesh,
        in_specs=(
            P(None, "lat", "lon"),
            P(None, ("lat", "lon")),
            P(None, ("lat", "lon")),
            P(("lat", "lon")),
            P(("lat", "lon")),
            P(),
            P(),
            P(),
            P(),
            P(),
            P(),
            P(),
            P(),
            P(),
            P(),
        ),
        out_specs=P(None, "lat", "lon"),
        check_vma=False,
    )
```

```python
import jax
import jax.numpy as jnp
from jax import lax
from jax.experimental import pallas as pl
from jax.experimental.pallas import tpu as pltpu
from jax.sharding import PartitionSpec as P

W = 4
SRC = 80
ROWS = 32
OBS_BLOCK = 512
GRID_ROWS = 384
CB = 64
RB = 8
BF = jnp.bfloat16
F = jnp.float32
MIB = 2**20
LAT_STATE = 9 * SRC
LAT_MSG = 9 * SRC + 3 * 256
LON_STATE = 2 * SRC
LON_MSG = 2 * SRC + 256
RIMS = 2 * SRC + 2 * 256

inverse_width = 1.0 / (2.0 * 1.5 * 1.5)


def lanes(rows):
    return lax.broadcasted_iota(jnp.int32, (rows, 128), 1)


def sums_kernel(count, row_base, vals_in, offs_in, cell_in, state_in, sums, up, down, vals, offs, cell, state, scaled, acc, sems):
    live_count = count[0]
    copies = [
        pltpu.make_async_copy(vals_in, vals, sems.at[0]),
        pltpu.make_async_copy(offs_in, offs, sems.at[1]),
        pltpu.make_async_copy(cell_in, cell, sems.at[2]),
        pltpu.make_async_copy(state_in.at[:, 0:8, :], state.at[:, 0:8, :], sems.at[3]),
        pltpu.make_async_copy(state_in.at[:, 16:24, :], state.at[:, 8:16, :], sems.at[4]),
    ]
    for copy in copies:
        copy.start()
    acc[...] = jnp.zeros(acc.shape, F)
    for copy in copies[:3]:
        copy.wait()

    def add_block(b, _):
        k0 = pl.multiple_of(b * OBS_BLOCK, OBS_BLOCK)
        ks = pl.ds(k0, OBS_BLOCK)
        where_cell = cell[:, ks]
        row = where_cell >> 7
        col = where_cell & 127
        slot = lax.broadcasted_iota(jnp.int32, (1, OBS_BLOCK), 1) + k0
        row = jnp.where(slot < live_count, row, -100)

        def weight(offset, place, centre, valid):
            apart = place - centre
            spread = offset - apart.astype(F) - 0.5
            inside = (jnp.abs(apart) <= W) & valid
            return jnp.where(inside, jnp.exp(-spread * spread * inverse_width), 0.0)

        place = lax.broadcasted_iota(jnp.int32, (ROWS, OBS_BLOCK), 0) - W
        on_grid = (place + row_base[0] >= 0) & (place + row_base[0] < GRID_ROWS)
        lat_weight = weight(offs[0:1, ks], place, row, on_grid)
        place = lax.broadcasted_iota(jnp.int32, (136, OBS_BLOCK), 0)
        first = weight(offs[1:2, ks], place, col, place < 128 + W)
        place = lax.broadcasted_iota(jnp.int32, (8, OBS_BLOCK), 0) - 8
        last = weight(offs[1:2, ks], place, col, place >= -W)
        lon_weight = jnp.concatenate([first, jnp.zeros((112, OBS_BLOCK), F), last], 0).astype(BF)
        ones = jnp.where(lax.broadcasted_iota(jnp.int32, (SRC - 64, OBS_BLOCK), 0) == 0, 1.0, 0.0)
        v = jnp.concatenate([vals[:, ks].astype(F), ones], 0)
        for p in range(ROWS):
            scaled[p * SRC:(p + 1) * SRC] = (v * lat_weight[p:p + 1]).astype(BF)
        for m in range(0, ROWS * SRC, 640):
            acc[m:m + 640] += lax.dot_general(
                scaled[m:m + 640], lon_weight, (((1,), (1,)), ((), ())), preferred_element_type=F)
        return 0

    lax.fori_loop(0, (live_count + OBS_BLOCK - 1) // OBS_BLOCK, add_block, 0)
    for copy in copies[3:]:
        copy.wait()
    for p in range(ROWS):
        sums[p] = acc[p * SRC:(p + 1) * SRC].astype(BF)
    for msg, first, state_tile, state_row in ((up, 0, 0, 0), (down, 24, 8, 5)):
        side = jnp.zeros((SRC, 128), F)
        for i in range(8):
            part = acc[(first + i) * SRC:(first + i + 1) * SRC]
            msg[i * SRC:(i + 1) * SRC] = part[:, :128].astype(BF)
            moved = pltpu.roll(part[:, 128:], i * 8 + 4, 1)
            side = jnp.where((lanes(SRC) >> 3) == i, moved, side)
        msg[8 * SRC:9 * SRC] = side.astype(BF)
        for c in range(0, 256, 16):
            x = jnp.swapaxes(state[c:c + 16, state_tile:state_tile + 8, :].astype(F), 0, 1).astype(BF)
            for j in range(3):
                msg[LAT_STATE + j * 256 + c:LAT_STATE + j * 256 + c + 16] = x[state_row + j]


def observation_sums(obs_values, obs_offsets, obs_cell, obs_count, row_base, state):
    S = pl.BlockSpec(memory_space=pltpu.SMEM)
    V = pl.BlockSpec(memory_space=pltpu.VMEM)
    shape = jax.ShapeDtypeStruct
    return pl.pallas_call(
        sums_kernel, name="observation_sums",
        out_shape=(shape((ROWS, SRC, 256), BF), shape((LAT_MSG, 128), BF), shape((LAT_MSG, 128), BF)),
        in_specs=[S, S] + [pl.BlockSpec(memory_space=pl.ANY)] * 4, out_specs=(V,) * 3,
        scratch_shapes=[
            pltpu.VMEM((64, 2048), BF), pltpu.VMEM((2, 2048), F), pltpu.VMEM((1, 2048), jnp.int32), pltpu.VMEM((256, 16, 128), BF),
            pltpu.VMEM((ROWS * SRC, OBS_BLOCK), BF), pltpu.VMEM((ROWS * SRC, 256), F), pltpu.SemaphoreType.DMA((5,)),
        ],
        compiler_params=pltpu.CompilerParams(vmem_limit_bytes=56 * MIB),
    )(obs_count, row_base, obs_values, obs_offsets, obs_cell.reshape(1, -1), state)


def place(p):
    return 15 - p % 16


def pack(packed, p, main, side):
    lane = lanes(SRC)
    k, shift = p // 16, place(p) * 8 + 4
    here = (lane >> 3) == place(p)
    packed[0][k] = jnp.where(here, pltpu.roll(jnp.where(lane < 4, main, side), shift, 1), packed[0][k])
    packed[1][k] = jnp.where(here, pltpu.roll(jnp.where(lane >= 124, main, side), shift, 1), packed[1][k])


def rows_kernel(state, sums, rows, rims):
    def turn(i, _):
        c0 = pl.multiple_of(i * 16, 16)
        rows[:, pl.ds(c0, 16), :] = jnp.swapaxes(state[pl.ds(c0, 16)].astype(F), 0, 1).astype(BF)
        return 0

    lax.fori_loop(0, 16, turn, 0)
    for c in range(0, 256, 64):
        packed = [jnp.zeros((64, 128), F) for _ in range(2)]
        for r in range(24):
            p = r + W
            moved = pltpu.roll(rows[r, c:c + 64, :].astype(F), place(p) * 8 + 4, 1)
            packed[p // 16] = jnp.where((lanes(64) >> 3) == place(p), moved, packed[p // 16])
        for k in range(2):
            rims[LON_STATE + k * 256 + c:LON_STATE + k * 256 + c + 64] = packed[k].astype(BF)
    packed = [[jnp.zeros((SRC, 128), F) for _ in range(2)] for _ in range(2)]
    for p in range(8, 24):
        pack(packed, p, sums[p, :, :128].astype(F), sums[p, :, 128:].astype(F))
    for k in range(2):
        rims[k * SRC:(k + 1) * SRC] = packed[0][k].astype(BF)
        rims[RIMS + k * SRC:RIMS + (k + 1) * SRC] = packed[1][k].astype(BF)


def state_rows(state, sums):
    shape = jax.ShapeDtypeStruct
    return pl.pallas_call(
        rows_kernel, name="state_rows", out_shape=(shape((24, 256, 128), BF), shape((RIMS + LON_STATE, 128), BF)),
        cost_estimate=pl.CostEstimate(flops=10**7, bytes_accessed=8 * 10**6, transcendentals=0),
        compiler_params=pltpu.CompilerParams(vmem_limit_bytes=16 * MIB),
    )(state, sums)


def edge_kernel(sums, rims, above, below, edge, left, right):
    lane = lanes(SRC)
    outer = (lane < 4) | (lane >= 124)
    packed = [[rims[first + k * SRC:first + (k + 1) * SRC].astype(F) for k in range(2)] for first in (0, RIMS)]
    for e in range(16):
        p = e if e < 8 else e + 16
        msg, i = (above, p) if p < 8 else (below, p - 24)
        moved = pltpu.roll(msg[8 * SRC:9 * SRC].astype(F), 124 - i * 8, 1)
        main = sums[p, :, :128].astype(F) + msg[i * SRC:(i + 1) * SRC].astype(F)
        side = sums[p, :, 128:].astype(F) + jnp.where(outer, moved, 0.0)
        edge[e] = main.astype(BF)
        pack(packed, p, main, side)
    for k in range(2):
        left[k * SRC:(k + 1) * SRC] = packed[0][k].astype(BF)
        right[k * SRC:(k + 1) * SRC] = packed[1][k].astype(BF)
    early = (lanes(64) & 7) < 4
    for c in range(0, 256, 64):
        halves = []
        for k, msg, first in ((0, above, 1), (1, below, 28)):
            at = LON_STATE + k * 256 + c
            out = rims[at:at + 64].astype(F)
            for j in range(3):
                p = first + j
                x = msg[LAT_STATE + j * 256 + c:LAT_STATE + j * 256 + c + 64].astype(F)
                out = jnp.where((lanes(64) >> 3) == place(p), pltpu.roll(x, place(p) * 8 + 4, 1), out)
            halves.append(out)
        at = slice(LON_STATE + c, LON_STATE + c + 64)
        left[at] = jnp.where(early, pltpu.roll(halves[1], 124, 1), halves[0]).astype(BF)
        right[at] = jnp.where(early, halves[0], pltpu.roll(halves[1], 4, 1)).astype(BF)


def edge_sums(sums, rims, above, below):
    shape = jax.ShapeDtypeStruct
    return pl.pallas_call(
        edge_kernel, name="edge_sums",
        out_shape=(shape((16, SRC, 128), BF), shape((LON_MSG, 128), BF), shape((LON_MSG, 128), BF)),
        compiler_params=pltpu.CompilerParams(vmem_limit_bytes=16 * MIB),
    )(sums, rims, above, below)


def prepare_kernel(taps, w_in, w_up, w_down, b1, toe, wi, w1, w2, b1c, smat, padded, base):
    smat[...] = shift_matrix()
    padded[...] = jnp.zeros(padded.shape, F)
    padded[0:65] = w_in[...].astype(F)
    wi[...] = padded[...].T.astype(BF)
    w1[...] = w_up[...].T
    w2[...] = w_down[...].T
    b1c[...] = b1[...].T
    base[...] = jnp.zeros(base.shape, F)
    for v in range(7):
        for u in range(7):
            base[32 * v + 1 + u:32 * v + 2 + u] = taps[u, v:v + 1]
    base[...] = base[...].T

    def step(i, _):
        rows = base[pl.ds(pl.multiple_of(i * 8, 8), 8), :]
        for k in range(8):
            parts = []
            for ln in range(2):
                b = jnp.broadcast_to(rows[k:k + 1, ln * 128:(ln + 1) * 128], (24, 128))
                parts.append(pltpu.roll(b, 0, 1, stride=1, stride_axis=0))
            y = jnp.concatenate(parts, 1).astype(BF)
            toe[i * 4 + k // 2, (k % 2) * 24:(k % 2) * 24 + 24, :] = y[:, :224]
        return 0

    lax.fori_loop(0, 32, step, 0)


def prepare(dw_weight, w_in, w_up, w_down, up_bias):
    shape = jax.ShapeDtypeStruct
    return pl.pallas_call(
        prepare_kernel, name="prepare",
        out_shape=(shape((128, 48, 224), BF), shape((256, SRC), BF), shape((1024, 256), BF), shape((256, 1024), BF), shape((128, 8), F), shape((256, 768), BF)),
        scratch_shapes=[pltpu.VMEM((SRC, 256), F), pltpu.VMEM((256, 256), F)],
        cost_estimate=pl.CostEstimate(flops=10**7, bytes_accessed=8 * 10**6, transcendentals=0),
        compiler_params=pltpu.CompilerParams(vmem_limit_bytes=16 * MIB),
    )(jnp.transpose(dw_weight, (1, 2, 0)), w_in, w_up, w_down, up_bias.reshape(8, 128))


def shift_matrix():
    lane = lax.broadcasted_iota(jnp.int32, (256, 768), 0)
    out = lax.broadcasted_iota(jnp.int32, (256, 768), 1)
    j = lane & 7
    col = jnp.where(lane < 128, lane, jnp.where(j < 4, j - 4, j + 124))
    k = out // 128
    d = jnp.where(k < 3, k - 3, k - 2)
    return jnp.where(col == out % 128 + d, 1.0, 0.0).astype(BF)


def encode_kernel(sums, edge, above, below, rows, wi, native, mixed):
    def encode(*cases):
        both = jnp.dot(wi[...], jnp.concatenate([main for _, main, _ in cases], 1), preferred_element_type=F)
        for n, (p, _, state) in enumerate(cases):
            mixed[p] = (both[:, n * 128:(n + 1) * 128] + state.astype(F)).astype(BF)

    mixed[0] = jnp.zeros((256, 128), BF)
    mixed[31] = jnp.zeros((256, 128), BF)
    for j in range(3):
        at = slice(LAT_STATE + j * 256, LAT_STATE + j * 256 + 256)
        encode((1 + j, edge[1 + j], above[at]), (28 + j, edge[12 + j], below[at]))

    def edge_row(j, _):
        encode((4 + j, edge[4 + j], rows[j]), (24 + j, edge[8 + j], rows[20 + j]))
        return 0

    def inner_row(j, _):
        encode((8 + j, sums[8 + j, :, :128], rows[4 + j]), (16 + j, sums[16 + j, :, :128], rows[12 + j]))
        return 0

    lax.fori_loop(0, 4, edge_row, 0)
    lax.fori_loop(0, 8, inner_row, 0)

    def turn(i, _):
        c0 = pl.multiple_of(i * CB, CB)
        native[pl.ds(c0, CB)] = jnp.swapaxes(mixed[:, pl.ds(c0, CB), :].astype(F), 0, 1).astype(BF)
        return 0

    lax.fori_loop(0, 256 // CB, turn, 0)


def encode(*arrays):
    return pl.pallas_call(
        encode_kernel, name="encode", out_shape=jax.ShapeDtypeStruct((256, ROWS, 128), BF),
        scratch_shapes=[pltpu.VMEM((ROWS, 256, 128), BF)],
        cost_estimate=pl.CostEstimate(flops=10**8, bytes_accessed=8 * 10**6, transcendentals=0),
        compiler_params=pltpu.CompilerParams(vmem_limit_bytes=20 * MIB),
    )(*arrays)


def block_kernel(dwb, gain, nbias, db, ls, partial, left, right, from_left, from_right,
                 toe, wi, w1, b1, w2, smat, out, native, sides, inward, mext, xs, filt, xbuf, obuf, result, sems):
    first = (lanes(SRC) & 7) < 4
    parts = []
    for k in range(2):
        at = slice(k * SRC, (k + 1) * SRC)
        a, b = from_left[at].astype(F), from_right[at].astype(F)
        parts.append(jnp.where(first, left[at].astype(F) + a, right[at].astype(F) + b))
        parts.append(jnp.where(first, b, a))
    both = jnp.dot(wi[...], jnp.concatenate(parts, 1).astype(BF), preferred_element_type=F)
    first = (lanes(256) & 7) < 4
    a, b = from_left[LON_STATE:LON_STATE + 256].astype(F), from_right[LON_STATE:LON_STATE + 256].astype(F)
    rims = (jnp.where(first, a, b), jnp.where(first, pltpu.roll(a, 124, 1), pltpu.roll(b, 4, 1)))
    for k in range(2):
        sides[:, k * 128:(k + 1) * 128] = (both[:, 2 * k * 128:(2 * k + 1) * 128] + rims[k]).astype(BF).astype(F)
        inward[:, k * 128:(k + 1) * 128] = both[:, (2 * k + 1) * 128:(2 * k + 2) * 128]
    slot = (lanes(16) >> 3) == 15 - lax.broadcasted_iota(jnp.int32, (16, 128), 0)
    outer = (lanes(16) < 4) | (lanes(16) >= 124)

    def filt_step(i, carry):
        pivot, s1, s2 = carry
        c0 = pl.multiple_of(i * CB, CB)
        side, more = sides[pl.ds(c0, CB)], inward[pl.ds(c0, CB)]
        for c in range(CB):
            for k in range(2):
                at = slice(c * 32 + k * 16, c * 32 + k * 16 + 16)
                ks = slice(k * 128, (k + 1) * 128)
                spread = jnp.broadcast_to(side[c:c + 1, ks], (16, 128))
                mext[at, 128:] = jnp.where(slot, spread, 0.0).astype(BF)
                moved = pltpu.roll(jnp.broadcast_to(more[c:c + 1, ks], (16, 128)), 4, 1, stride=8, stride_axis=0)
                main = (partial[c0 + c, k * 16:k * 16 + 16].astype(F) + jnp.where(outer, moved, 0.0)).astype(BF)
                mext[at, :128] = main
                native[c0 + c, k * 16:k * 16 + 16] = main
                xs[c // 2, 96 + k * 16:112 + k * 16, (c % 2) * 128:(c % 2) * 128 + 128] = main
        for j in range(3):
            z = jnp.dot(mext[...], smat[:, j * 256:(j + 1) * 256], preferred_element_type=F).astype(BF)
            for half in range(2):
                k = 2 * j + half
                v = k if k < 3 else k + 1
                zz = z[:, half * 128:(half + 1) * 128]
                for c in range(CB):
                    xs[c // 2, v * 32:(v + 1) * 32, (c % 2) * 128:(c % 2) * 128 + 128] = zz[c * 32:(c + 1) * 32]
        for k in range(CB // 2):
            o = jnp.dot(toe[i * (CB // 2) + k], xs[k], preferred_element_type=F)
            for c, y in ((c0 + 2 * k, o[:24, :128]), (c0 + 2 * k + 1, o[24:, 128:])):
                y = y + dwb[c]
                if k == 0:
                    pivot = jnp.where(c == 0, y, pivot)
                y = y - pivot
                filt[c] = y
                s1 = s1 + y
                s2 = s2 + y * y
        return pivot, s1, s2

    zero = jnp.zeros((24, 128), F)
    _, s1, s2 = lax.fori_loop(0, 256 // CB, filt_step, (zero, zero, zero))
    mean = s1 * (1.0 / 256)
    rstd = lax.rsqrt(jnp.maximum(s2 * (1.0 / 256) - mean * mean, 0.0) + 1e-6)

    def norm_step(i, _):
        c0 = pl.multiple_of(i * 16, 16)
        ys = [((filt[c0 + k] - mean) * rstd) * gain[c0 + k] + nbias[c0 + k] for k in range(16)]
        xbuf[:, pl.ds(c0, 16), :] = jnp.swapaxes(jnp.stack(ys, 0), 0, 1).astype(BF)
        return 0

    lax.fori_loop(0, 16, norm_step, 0)

    def mlp_step(i, _):
        x = jnp.concatenate([xbuf[i * RB + k] for k in range(RB)], 1)
        h = jnp.dot(w1[...], x, preferred_element_type=F)
        gs = []
        for k in range(8):
            hk = h[k * 128:(k + 1) * 128] + b1[:, k:k + 1]
            gs.append(((0.5 * hk) * (1.0 + lax.erf(hk * 0.7071067811865476))).astype(BF))
        o = jnp.dot(w2[...], jnp.concatenate(gs, 0), preferred_element_type=F)
        for k in range(RB):
            obuf[i * RB + k] = o[:, k * 128:(k + 1) * 128]
        return 0

    lax.fori_loop(0, 24 // RB, mlp_step, 0)

    def out_step(i, _):
        c0 = pl.multiple_of(i * 16, 16)
        o = jnp.swapaxes(obuf[:, pl.ds(c0, 16), :], 0, 1)
        m = native[pl.ds(c0, 16)].astype(F)
        for k in range(16):
            result[c0 + k] = (m[k, 4:28] + (o[k] + db[c0 + k]) * ls[c0 + k]).astype(BF)
        return 0

    copies = []
    for n in range(4):
        lax.fori_loop(4 * n, 4 * n + 4, out_step, 0)
        at = slice(64 * n, 64 * n + 64)
        copies.append(pltpu.make_async_copy(result.at[at], out.at[at], sems.at[n]))
        copies[-1].start()
    for copy in copies:
        copy.wait()


def block(arrays, vectors):
    S = pl.BlockSpec(memory_space=pltpu.SMEM)
    V = pl.BlockSpec(memory_space=pltpu.VMEM)
    return pl.pallas_call(
        block_kernel, name="block", out_shape=jax.ShapeDtypeStruct((256, 24, 128), BF),
        in_specs=[S] * len(vectors) + [V] * len(arrays), out_specs=pl.BlockSpec(memory_space=pl.ANY),
        scratch_shapes=[
            pltpu.VMEM((256, ROWS, 128), BF), pltpu.VMEM((256, 256), F), pltpu.VMEM((256, 256), F),
            pltpu.VMEM((CB * 32, 256), BF), pltpu.VMEM((CB // 2, 224, 256), BF),
            pltpu.VMEM((256, 24, 128), F), pltpu.VMEM((24, 256, 128), BF), pltpu.VMEM((24, 256, 128), F),
            pltpu.VMEM((256, 24, 128), BF), pltpu.SemaphoreType.DMA((4,)),
        ],
        compiler_params=pltpu.CompilerParams(vmem_limit_bytes=30 * MIB),
    )(*vectors, *arrays)


def exchange(to_lower, to_upper, axis, wrap):
    size = lax.axis_size(axis)
    up = [(i, (i + 1) % size) for i in range(size if wrap else size - 1)]
    down = [(j, i) for i, j in up]
    return lax.ppermute(to_upper, axis, up), lax.ppermute(to_lower, axis, down)


def local(state, obs_values, obs_offsets, obs_cell, obs_count, w_in, dw_weight, dw_bias, norm_gain, norm_bias,
          w_up, up_bias, w_down, down_bias, layer_scale):
    row_base = (lax.axis_index("lat") * state.shape[1]).astype(jnp.int32).reshape(1)
    sums, up, down = observation_sums(obs_values, obs_offsets, obs_cell, obs_count, row_base, state)
    above, below = exchange(up, down, "lat", False)
    rows, rims = state_rows(state, sums)
    dw_later, w_up_later, w_down_later, _ = lax.optimization_barrier((dw_weight, w_up, w_down, rows))
    weights = prepare(dw_later, w_in, w_up_later, w_down_later, up_bias)
    rims, (toe, wi, w1, w2, b1, smat) = lax.optimization_barrier((rims, weights))
    edge, left, right = edge_sums(sums, rims, above, below)
    from_left, from_right = exchange(left, right, "lon", True)
    partial = encode(sums, edge, above, below, rows, wi)
    return block(
        (partial, left, right, from_left, from_right, toe, wi, w1, b1, w2, smat),
        (dw_bias, norm_gain, norm_bias, down_bias, layer_scale),
    )


def solution(mesh):
    return jax.shard_map(
        local,
        mesh=mesh,
        in_specs=(
            P(None, "lat", "lon"),
            P(None, ("lat", "lon")),
            P(None, ("lat", "lon")),
            P(("lat", "lon")),
            P(("lat", "lon")),
            P(),
            P(),
            P(),
            P(),
            P(),
            P(),
            P(),
            P(),
            P(),
            P(),
        ),
        out_specs=P(None, "lat", "lon"),
        check_vma=False,
    )
```

```python
import jax
import jax.numpy as jnp
from jax import lax
from jax.experimental import pallas as pl
from jax.experimental.pallas import tpu as pltpu
from jax.sharding import PartitionSpec as P

W = 4
SRC = 80
ROWS = 32
OBS_BLOCK = 512
GRID_ROWS = 384
CB = 64
RB = 8
BF = jnp.bfloat16
F = jnp.float32
MIB = 2**20
LAT_STATE = 9 * SRC
LAT_MSG = 9 * SRC + 3 * 256
LON_STATE = 2 * SRC
LON_MSG = 2 * SRC + 256
RIMS = 2 * SRC + 2 * 256

inverse_width = 1.0 / (2.0 * 1.5 * 1.5)


def lanes(rows):
    return lax.broadcasted_iota(jnp.int32, (rows, 128), 1)


def even(index):
    return (index[0] & 1) == 0


def pick(condition, a, b, at):
    return jnp.where(condition, a[at].astype(F), b[at].astype(F))


def sums_kernel(count, lat, vals_in, offs_in, cell_in, state_in, sums, out_a, out_b, vals, offs, cell, state, scaled, acc, sems):
    live_count = count[0]
    row_base = lat[0] * 24
    copies = [
        pltpu.make_async_copy(vals_in, vals, sems.at[0]),
        pltpu.make_async_copy(offs_in, offs, sems.at[1]),
        pltpu.make_async_copy(cell_in, cell, sems.at[2]),
        pltpu.make_async_copy(state_in.at[:, 0:8, :], state.at[:, 0:8, :], sems.at[3]),
        pltpu.make_async_copy(state_in.at[:, 16:24, :], state.at[:, 8:16, :], sems.at[4]),
    ]
    for copy in copies:
        copy.start()
    acc[...] = jnp.zeros(acc.shape, F)
    for copy in copies[:3]:
        copy.wait()

    def add_block(b, _):
        k0 = pl.multiple_of(b * OBS_BLOCK, OBS_BLOCK)
        ks = pl.ds(k0, OBS_BLOCK)
        where_cell = cell[:, ks]
        row = where_cell >> 7
        col = where_cell & 127
        slot = lax.broadcasted_iota(jnp.int32, (1, OBS_BLOCK), 1) + k0
        row = jnp.where(slot < live_count, row, -100)

        def weight(offset, place, centre, valid):
            apart = place - centre
            spread = offset - apart.astype(F) - 0.5
            inside = (jnp.abs(apart) <= W) & valid
            return jnp.where(inside, jnp.exp(-spread * spread * inverse_width), 0.0)

        place = lax.broadcasted_iota(jnp.int32, (ROWS, OBS_BLOCK), 0) - W
        on_grid = (place + row_base >= 0) & (place + row_base < GRID_ROWS)
        lat_weight = weight(offs[0:1, ks], place, row, on_grid)
        place = lax.broadcasted_iota(jnp.int32, (136, OBS_BLOCK), 0)
        first = weight(offs[1:2, ks], place, col, place < 128 + W)
        place = lax.broadcasted_iota(jnp.int32, (8, OBS_BLOCK), 0) - 8
        last = weight(offs[1:2, ks], place, col, place >= -W)
        lon_weight = jnp.concatenate([first, jnp.zeros((112, OBS_BLOCK), F), last], 0).astype(BF)
        ones = jnp.where(lax.broadcasted_iota(jnp.int32, (SRC - 64, OBS_BLOCK), 0) == 0, 1.0, 0.0)
        v = jnp.concatenate([vals[:, ks].astype(F), ones], 0)
        for p in range(ROWS):
            scaled[p * SRC:(p + 1) * SRC] = (v * lat_weight[p:p + 1]).astype(BF)
        for m in range(0, ROWS * SRC, 640):
            acc[m:m + 640] += lax.dot_general(
                scaled[m:m + 640], lon_weight, (((1,), (1,)), ((), ())), preferred_element_type=F)
        return 0

    lax.fori_loop(0, (live_count + OBS_BLOCK - 1) // OBS_BLOCK, add_block, 0)
    for copy in copies[3:]:
        copy.wait()
    for p in range(ROWS):
        sums[p] = acc[p * SRC:(p + 1) * SRC].astype(BF)
    def fill(up, down):
        for msg, first, state_tile, state_row in ((up, 0, 0, 0), (down, 24, 8, 5)):
            side = jnp.zeros((SRC, 128), F)
            for i in range(8):
                part = acc[(first + i) * SRC:(first + i + 1) * SRC]
                msg[i * SRC:(i + 1) * SRC] = part[:, :128].astype(BF)
                moved = pltpu.roll(part[:, 128:], i * 8 + 4, 1)
                side = jnp.where((lanes(SRC) >> 3) == i, moved, side)
            msg[8 * SRC:9 * SRC] = side.astype(BF)
            for c in range(0, 256, 16):
                x = jnp.swapaxes(state[c:c + 16, state_tile:state_tile + 8, :].astype(F), 0, 1).astype(BF)
                for j in range(3):
                    msg[LAT_STATE + j * 256 + c:LAT_STATE + j * 256 + c + 16] = x[state_row + j]

    @pl.when(even(lat))
    def _():
        fill(out_b, out_a)

    @pl.when(jnp.logical_not(even(lat)))
    def _():
        fill(out_a, out_b)


def observation_sums(obs_values, obs_offsets, obs_cell, obs_count, lat, state):
    S = pl.BlockSpec(memory_space=pltpu.SMEM)
    V = pl.BlockSpec(memory_space=pltpu.VMEM)
    shape = jax.ShapeDtypeStruct
    return pl.pallas_call(
        sums_kernel, name="observation_sums",
        out_shape=(shape((ROWS, SRC, 256), BF), shape((LAT_MSG, 128), BF), shape((LAT_MSG, 128), BF)),
        in_specs=[S, S] + [pl.BlockSpec(memory_space=pl.ANY)] * 4, out_specs=(V,) * 3,
        scratch_shapes=[
            pltpu.VMEM((64, 2048), BF), pltpu.VMEM((2, 2048), F), pltpu.VMEM((1, 2048), jnp.int32), pltpu.VMEM((256, 16, 128), BF),
            pltpu.VMEM((ROWS * SRC, OBS_BLOCK), BF), pltpu.VMEM((ROWS * SRC, 256), F), pltpu.SemaphoreType.DMA((5,)),
        ],
        compiler_params=pltpu.CompilerParams(vmem_limit_bytes=56 * MIB),
    )(obs_count, lat, obs_values, obs_offsets, obs_cell.reshape(1, -1), state)


def place(p):
    return 15 - p % 16


def pack(packed, p, main, side):
    lane = lanes(SRC)
    k, shift = p // 16, place(p) * 8 + 4
    here = (lane >> 3) == place(p)
    packed[0][k] = jnp.where(here, pltpu.roll(jnp.where(lane < 4, main, side), shift, 1), packed[0][k])
    packed[1][k] = jnp.where(here, pltpu.roll(jnp.where(lane >= 124, main, side), shift, 1), packed[1][k])


def rows_kernel(state, sums, rows, rims):
    def turn(i, _):
        c0 = pl.multiple_of(i * 16, 16)
        rows[:, pl.ds(c0, 16), :] = jnp.swapaxes(state[pl.ds(c0, 16)].astype(F), 0, 1).astype(BF)
        return 0

    lax.fori_loop(0, 16, turn, 0)
    for c in range(0, 256, 64):
        packed = [jnp.zeros((64, 128), F) for _ in range(2)]
        for r in range(24):
            p = r + W
            moved = pltpu.roll(rows[r, c:c + 64, :].astype(F), place(p) * 8 + 4, 1)
            packed[p // 16] = jnp.where((lanes(64) >> 3) == place(p), moved, packed[p // 16])
        for k in range(2):
            rims[LON_STATE + k * 256 + c:LON_STATE + k * 256 + c + 64] = packed[k].astype(BF)
    packed = [[jnp.zeros((SRC, 128), F) for _ in range(2)] for _ in range(2)]
    for p in range(8, 24):
        pack(packed, p, sums[p, :, :128].astype(F), sums[p, :, 128:].astype(F))
    for k in range(2):
        rims[k * SRC:(k + 1) * SRC] = packed[0][k].astype(BF)
        rims[RIMS + k * SRC:RIMS + (k + 1) * SRC] = packed[1][k].astype(BF)


def state_rows(state, sums):
    shape = jax.ShapeDtypeStruct
    return pl.pallas_call(
        rows_kernel, name="state_rows", out_shape=(shape((24, 256, 128), BF), shape((RIMS + LON_STATE, 128), BF)),
        cost_estimate=pl.CostEstimate(flops=10**7, bytes_accessed=8 * 10**6, transcendentals=0),
        compiler_params=pltpu.CompilerParams(vmem_limit_bytes=16 * MIB),
    )(state, sums)


def edge_kernel(lat, lon, sums, rims, in_a, in_b, edge, out_a, out_b):
    lat_even, lon_even = even(lat), even(lon)
    above = lambda at: pick(lat_even, in_b, in_a, at)
    below = lambda at: pick(lat_even, in_a, in_b, at)

    def store(at, left, right):
        out_a[at] = jnp.where(lon_even, right, left).astype(BF)
        out_b[at] = jnp.where(lon_even, left, right).astype(BF)

    lane = lanes(SRC)
    outer = (lane < 4) | (lane >= 124)
    packed = [[rims[first + k * SRC:first + (k + 1) * SRC].astype(F) for k in range(2)] for first in (0, RIMS)]
    for e in range(16):
        p = e if e < 8 else e + 16
        msg, i = (above, p) if p < 8 else (below, p - 24)
        moved = pltpu.roll(msg(slice(8 * SRC, 9 * SRC)), 124 - i * 8, 1)
        main = sums[p, :, :128].astype(F) + msg(slice(i * SRC, (i + 1) * SRC))
        side = sums[p, :, 128:].astype(F) + jnp.where(outer, moved, 0.0)
        edge[e] = main.astype(BF)
        pack(packed, p, main, side)
    for k in range(2):
        store(slice(k * SRC, (k + 1) * SRC), packed[0][k], packed[1][k])
    early = (lanes(64) & 7) < 4
    for c in range(0, 256, 64):
        halves = []
        for k, msg, first in ((0, above, 1), (1, below, 28)):
            at = LON_STATE + k * 256 + c
            out = rims[at:at + 64].astype(F)
            for j in range(3):
                p = first + j
                x = msg(slice(LAT_STATE + j * 256 + c, LAT_STATE + j * 256 + c + 64))
                out = jnp.where((lanes(64) >> 3) == place(p), pltpu.roll(x, place(p) * 8 + 4, 1), out)
            halves.append(out)
        at = slice(LON_STATE + c, LON_STATE + c + 64)
        store(
            at,
            jnp.where(early, pltpu.roll(halves[1], 124, 1), halves[0]),
            jnp.where(early, halves[0], pltpu.roll(halves[1], 4, 1)),
        )


def edge_sums(*arrays):
    shape = jax.ShapeDtypeStruct
    return pl.pallas_call(
        edge_kernel, name="edge_sums", in_specs=[pl.BlockSpec(memory_space=pltpu.SMEM)] * 2 + [pl.BlockSpec(memory_space=pltpu.VMEM)] * 4,
        out_shape=(shape((16, SRC, 128), BF), shape((LON_MSG, 128), BF), shape((LON_MSG, 128), BF)),
        compiler_params=pltpu.CompilerParams(vmem_limit_bytes=16 * MIB),
    )(*arrays)


def prepare_kernel(taps, w_in, w_up, w_down, b1, toe, wi, w1, w2, b1c, smat, padded, base):
    smat[...] = shift_matrix()
    padded[...] = jnp.zeros(padded.shape, F)
    padded[0:65] = w_in[...].astype(F)
    wi[...] = padded[...].T.astype(BF)
    w1[...] = w_up[...].T
    w2[...] = w_down[...].T
    b1c[...] = b1[...].T
    base[...] = jnp.zeros(base.shape, F)
    for v in range(7):
        for u in range(7):
            base[32 * v + 1 + u:32 * v + 2 + u] = taps[u, v:v + 1]
    base[...] = base[...].T

    def step(i, _):
        rows = base[pl.ds(pl.multiple_of(i * 8, 8), 8), :]
        for k in range(8):
            parts = []
            for ln in range(2):
                b = jnp.broadcast_to(rows[k:k + 1, ln * 128:(ln + 1) * 128], (24, 128))
                parts.append(pltpu.roll(b, 0, 1, stride=1, stride_axis=0))
            y = jnp.concatenate(parts, 1).astype(BF)
            toe[i * 4 + k // 2, (k % 2) * 24:(k % 2) * 24 + 24, :] = y[:, :224]
        return 0

    lax.fori_loop(0, 32, step, 0)


def prepare(dw_weight, w_in, w_up, w_down, up_bias):
    shape = jax.ShapeDtypeStruct
    return pl.pallas_call(
        prepare_kernel, name="prepare",
        out_shape=(shape((128, 48, 224), BF), shape((256, SRC), BF), shape((1024, 256), BF), shape((256, 1024), BF), shape((128, 8), F), shape((256, 768), BF)),
        scratch_shapes=[pltpu.VMEM((SRC, 256), F), pltpu.VMEM((256, 256), F)],
        cost_estimate=pl.CostEstimate(flops=10**7, bytes_accessed=8 * 10**6, transcendentals=0),
        compiler_params=pltpu.CompilerParams(vmem_limit_bytes=16 * MIB),
    )(jnp.transpose(dw_weight, (1, 2, 0)), w_in, w_up, w_down, up_bias.reshape(8, 128))


def shift_matrix():
    lane = lax.broadcasted_iota(jnp.int32, (256, 768), 0)
    out = lax.broadcasted_iota(jnp.int32, (256, 768), 1)
    j = lane & 7
    col = jnp.where(lane < 128, lane, jnp.where(j < 4, j - 4, j + 124))
    k = out // 128
    d = jnp.where(k < 3, k - 3, k - 2)
    return jnp.where(col == out % 128 + d, 1.0, 0.0).astype(BF)


def encode_kernel(lat, sums, edge, in_a, in_b, rows, wi, native, mixed):
    lat_even = even(lat)

    def encode(*cases):
        both = jnp.dot(wi[...], jnp.concatenate([main for _, main, _ in cases], 1), preferred_element_type=F)
        for n, (p, _, state) in enumerate(cases):
            mixed[p] = (both[:, n * 128:(n + 1) * 128] + state.astype(F)).astype(BF)

    mixed[0] = jnp.zeros((256, 128), BF)
    mixed[31] = jnp.zeros((256, 128), BF)
    for j in range(3):
        at = slice(LAT_STATE + j * 256, LAT_STATE + j * 256 + 256)
        encode((1 + j, edge[1 + j], pick(lat_even, in_b, in_a, at)), (28 + j, edge[12 + j], pick(lat_even, in_a, in_b, at)))

    def edge_row(j, _):
        encode((4 + j, edge[4 + j], rows[j]), (24 + j, edge[8 + j], rows[20 + j]))
        return 0

    def inner_row(j, _):
        encode((8 + j, sums[8 + j, :, :128], rows[4 + j]), (16 + j, sums[16 + j, :, :128], rows[12 + j]))
        return 0

    lax.fori_loop(0, 4, edge_row, 0)
    lax.fori_loop(0, 8, inner_row, 0)

    def turn(i, _):
        c0 = pl.multiple_of(i * CB, CB)
        native[pl.ds(c0, CB)] = jnp.swapaxes(mixed[:, pl.ds(c0, CB), :].astype(F), 0, 1).astype(BF)
        return 0

    lax.fori_loop(0, 256 // CB, turn, 0)


def encode(*arrays):
    return pl.pallas_call(
        encode_kernel, name="encode", in_specs=[pl.BlockSpec(memory_space=pltpu.SMEM)] + [pl.BlockSpec(memory_space=pltpu.VMEM)] * 6,
        out_shape=jax.ShapeDtypeStruct((256, ROWS, 128), BF),
        scratch_shapes=[pltpu.VMEM((ROWS, 256, 128), BF)],
        cost_estimate=pl.CostEstimate(flops=10**8, bytes_accessed=8 * 10**6, transcendentals=0),
        compiler_params=pltpu.CompilerParams(vmem_limit_bytes=20 * MIB),
    )(*arrays)


def block_kernel(lon, dwb, gain, nbias, db, ls, partial, out_a, out_b, in_a, in_b,
                 toe, wi, w1, b1, w2, smat, out, native, sides, inward, mext, xs, filt, xbuf, obuf, result, sems):
    lon_even = even(lon)
    first = (lanes(SRC) & 7) < 4
    parts = []
    for k in range(2):
        at = slice(k * SRC, (k + 1) * SRC)
        a, b = pick(lon_even, in_b, in_a, at), pick(lon_even, in_a, in_b, at)
        parts.append(jnp.where(first, pick(lon_even, out_b, out_a, at) + a, pick(lon_even, out_a, out_b, at) + b))
        parts.append(jnp.where(first, b, a))
    both = jnp.dot(wi[...], jnp.concatenate(parts, 1).astype(BF), preferred_element_type=F)
    first = (lanes(256) & 7) < 4
    at = slice(LON_STATE, LON_STATE + 256)
    a, b = pick(lon_even, in_b, in_a, at), pick(lon_even, in_a, in_b, at)
    rims = (jnp.where(first, a, b), jnp.where(first, pltpu.roll(a, 124, 1), pltpu.roll(b, 4, 1)))
    for k in range(2):
        sides[:, k * 128:(k + 1) * 128] = (both[:, 2 * k * 128:(2 * k + 1) * 128] + rims[k]).astype(BF).astype(F)
        inward[:, k * 128:(k + 1) * 128] = both[:, (2 * k + 1) * 128:(2 * k + 2) * 128]
    slot = (lanes(16) >> 3) == 15 - lax.broadcasted_iota(jnp.int32, (16, 128), 0)
    outer = (lanes(16) < 4) | (lanes(16) >= 124)

    def filt_step(i, carry):
        pivot, s1, s2 = carry
        c0 = pl.multiple_of(i * CB, CB)
        side, more = sides[pl.ds(c0, CB)], inward[pl.ds(c0, CB)]
        for c in range(CB):
            for k in range(2):
                at = slice(c * 32 + k * 16, c * 32 + k * 16 + 16)
                ks = slice(k * 128, (k + 1) * 128)
                spread = jnp.broadcast_to(side[c:c + 1, ks], (16, 128))
                mext[at, 128:] = jnp.where(slot, spread, 0.0).astype(BF)
                moved = pltpu.roll(jnp.broadcast_to(more[c:c + 1, ks], (16, 128)), 4, 1, stride=8, stride_axis=0)
                main = (partial[c0 + c, k * 16:k * 16 + 16].astype(F) + jnp.where(outer, moved, 0.0)).astype(BF)
                mext[at, :128] = main
                native[c0 + c, k * 16:k * 16 + 16] = main
                xs[c // 2, 96 + k * 16:112 + k * 16, (c % 2) * 128:(c % 2) * 128 + 128] = main
        for j in range(3):
            z = jnp.dot(mext[...], smat[:, j * 256:(j + 1) * 256], preferred_element_type=F).astype(BF)
            for half in range(2):
                k = 2 * j + half
                v = k if k < 3 else k + 1
                zz = z[:, half * 128:(half + 1) * 128]
                for c in range(CB):
                    xs[c // 2, v * 32:(v + 1) * 32, (c % 2) * 128:(c % 2) * 128 + 128] = zz[c * 32:(c + 1) * 32]
        for k in range(CB // 2):
            o = jnp.dot(toe[i * (CB // 2) + k], xs[k], preferred_element_type=F)
            for c, y in ((c0 + 2 * k, o[:24, :128]), (c0 + 2 * k + 1, o[24:, 128:])):
                y = y + dwb[c]
                if k == 0:
                    pivot = jnp.where(c == 0, y, pivot)
                y = y - pivot
                filt[c] = y
                s1 = s1 + y
                s2 = s2 + y * y
        return pivot, s1, s2

    zero = jnp.zeros((24, 128), F)
    _, s1, s2 = lax.fori_loop(0, 256 // CB, filt_step, (zero, zero, zero))
    mean = s1 * (1.0 / 256)
    rstd = lax.rsqrt(jnp.maximum(s2 * (1.0 / 256) - mean * mean, 0.0) + 1e-6)

    def norm_step(i, _):
        c0 = pl.multiple_of(i * 16, 16)
        ys = [((filt[c0 + k] - mean) * rstd) * gain[c0 + k] + nbias[c0 + k] for k in range(16)]
        xbuf[:, pl.ds(c0, 16), :] = jnp.swapaxes(jnp.stack(ys, 0), 0, 1).astype(BF)
        return 0

    lax.fori_loop(0, 16, norm_step, 0)

    def mlp_step(i, _):
        x = jnp.concatenate([xbuf[i * RB + k] for k in range(RB)], 1)
        h = jnp.dot(w1[...], x, preferred_element_type=F)
        gs = []
        for k in range(8):
            hk = h[k * 128:(k + 1) * 128] + b1[:, k:k + 1]
            gs.append(((0.5 * hk) * (1.0 + lax.erf(hk * 0.7071067811865476))).astype(BF))
        o = jnp.dot(w2[...], jnp.concatenate(gs, 0), preferred_element_type=F)
        for k in range(RB):
            obuf[i * RB + k] = o[:, k * 128:(k + 1) * 128]
        return 0

    lax.fori_loop(0, 24 // RB, mlp_step, 0)

    def out_step(i, _):
        c0 = pl.multiple_of(i * 16, 16)
        o = jnp.swapaxes(obuf[:, pl.ds(c0, 16), :], 0, 1)
        m = native[pl.ds(c0, 16)].astype(F)
        for k in range(16):
            result[c0 + k] = (m[k, 4:28] + (o[k] + db[c0 + k]) * ls[c0 + k]).astype(BF)
        return 0

    copies = []
    for n in range(4):
        lax.fori_loop(4 * n, 4 * n + 4, out_step, 0)
        at = slice(64 * n, 64 * n + 64)
        copies.append(pltpu.make_async_copy(result.at[at], out.at[at], sems.at[n]))
        copies[-1].start()
    for copy in copies:
        copy.wait()


def block(arrays, vectors):
    S = pl.BlockSpec(memory_space=pltpu.SMEM)
    V = pl.BlockSpec(memory_space=pltpu.VMEM)
    return pl.pallas_call(
        block_kernel, name="block", out_shape=jax.ShapeDtypeStruct((256, 24, 128), BF),
        in_specs=[S] * len(vectors) + [V] * len(arrays), out_specs=pl.BlockSpec(memory_space=pl.ANY),
        scratch_shapes=[
            pltpu.VMEM((256, ROWS, 128), BF), pltpu.VMEM((256, 256), F), pltpu.VMEM((256, 256), F),
            pltpu.VMEM((CB * 32, 256), BF), pltpu.VMEM((CB // 2, 224, 256), BF),
            pltpu.VMEM((256, 24, 128), F), pltpu.VMEM((24, 256, 128), BF), pltpu.VMEM((24, 256, 128), F),
            pltpu.VMEM((256, 24, 128), BF), pltpu.SemaphoreType.DMA((4,)),
        ],
        compiler_params=pltpu.CompilerParams(vmem_limit_bytes=30 * MIB),
    )(*vectors, *arrays)


def exchange(a, b, axis, wrap):
    size = lax.axis_size(axis)
    first = [(i, i + 1) for i in range(0, size, 2)]
    second = [(i, (i + 1) % size) for i in range(1, size if wrap else size - 1, 2)]
    swap = lambda x, pairs: lax.ppermute(x, axis, pairs + [(j, i) for i, j in pairs])
    return swap(a, first), swap(b, second)


def local(state, obs_values, obs_offsets, obs_cell, obs_count, w_in, dw_weight, dw_bias, norm_gain, norm_bias,
          w_up, up_bias, w_down, down_bias, layer_scale):
    lat = lax.axis_index("lat").astype(jnp.int32).reshape(1)
    lon = lax.axis_index("lon").astype(jnp.int32).reshape(1)
    sums, lat_a, lat_b = observation_sums(obs_values, obs_offsets, obs_cell, obs_count, lat, state)
    lat_a, lat_b = exchange(lat_a, lat_b, "lat", False)
    rows, rims = state_rows(state, sums)
    dw_later, w_up_later, w_down_later, _ = lax.optimization_barrier((dw_weight, w_up, w_down, rows))
    weights = prepare(dw_later, w_in, w_up_later, w_down_later, up_bias)
    rims, (toe, wi, w1, w2, b1, smat) = lax.optimization_barrier((rims, weights))
    edge, lon_a, lon_b = edge_sums(lat, lon, sums, rims, lat_a, lat_b)
    from_a, from_b = exchange(lon_a, lon_b, "lon", True)
    partial = encode(lat, sums, edge, lat_a, lat_b, rows, wi)
    return block(
        (partial, lon_a, lon_b, from_a, from_b, toe, wi, w1, b1, w2, smat),
        (lon, dw_bias, norm_gain, norm_bias, down_bias, layer_scale),
    )


def solution(mesh):
    return jax.shard_map(
        local,
        mesh=mesh,
        in_specs=(
            P(None, "lat", "lon"),
            P(None, ("lat", "lon")),
            P(None, ("lat", "lon")),
            P(("lat", "lon")),
            P(("lat", "lon")),
            P(),
            P(),
            P(),
            P(),
            P(),
            P(),
            P(),
            P(),
            P(),
            P(),
        ),
        out_specs=P(None, "lat", "lon"),
        check_vma=False,
    )
```

```python
import jax
import jax.numpy as jnp
from jax import lax
from jax.experimental import pallas as pl
from jax.experimental.pallas import tpu as pltpu
from jax.sharding import PartitionSpec as P

W = 4
SRC = 80
ROWS = 32
OBS_BLOCK = 512
GRID_ROWS = 384
CB = 128
RB = 8
BF = jnp.bfloat16
F = jnp.float32
MIB = 2**20
LAT_STATE = 9 * SRC
LAT_MSG = 9 * SRC + 3 * 256
LON_STATE = 2 * SRC
LON_MSG = 2 * SRC + 256
RIMS = 2 * SRC + 2 * 256

inverse_width = 1.0 / (2.0 * 1.5 * 1.5)


def lanes(rows):
    return lax.broadcasted_iota(jnp.int32, (rows, 128), 1)


def even(index):
    return (index[0] & 1) == 0


def pick(condition, a, b, at):
    return jnp.where(condition, a[at].astype(F), b[at].astype(F))


def sums_kernel(count, lat, vals_in, offs_in, cell_in, state_in, sums, out_a, out_b, vals, offs, cell, state, scaled, acc, sems):
    live_count = count[0]
    row_base = lat[0] * 24
    copies = [
        pltpu.make_async_copy(vals_in, vals, sems.at[0]),
        pltpu.make_async_copy(offs_in, offs, sems.at[1]),
        pltpu.make_async_copy(cell_in, cell, sems.at[2]),
        pltpu.make_async_copy(state_in.at[:, 0:8, :], state.at[:, 0:8, :], sems.at[3]),
        pltpu.make_async_copy(state_in.at[:, 16:24, :], state.at[:, 8:16, :], sems.at[4]),
    ]
    for copy in copies:
        copy.start()
    acc[...] = jnp.zeros(acc.shape, F)
    for copy in copies[:3]:
        copy.wait()

    def add_block(b, _):
        k0 = pl.multiple_of(b * OBS_BLOCK, OBS_BLOCK)
        ks = pl.ds(k0, OBS_BLOCK)
        where_cell = cell[:, ks]
        row = where_cell >> 7
        col = where_cell & 127
        slot = lax.broadcasted_iota(jnp.int32, (1, OBS_BLOCK), 1) + k0
        row = jnp.where(slot < live_count, row, -100)

        def weight(offset, place, centre, valid):
            apart = place - centre
            spread = offset - apart.astype(F) - 0.5
            inside = (jnp.abs(apart) <= W) & valid
            return jnp.where(inside, jnp.exp(-spread * spread * inverse_width), 0.0)

        place = lax.broadcasted_iota(jnp.int32, (ROWS, OBS_BLOCK), 0) - W
        on_grid = (place + row_base >= 0) & (place + row_base < GRID_ROWS)
        lat_weight = weight(offs[0:1, ks], place, row, on_grid)
        place = lax.broadcasted_iota(jnp.int32, (136, OBS_BLOCK), 0)
        first = weight(offs[1:2, ks], place, col, place < 128 + W)
        place = lax.broadcasted_iota(jnp.int32, (8, OBS_BLOCK), 0) - 8
        last = weight(offs[1:2, ks], place, col, place >= -W)
        lon_weight = jnp.concatenate([first, jnp.zeros((112, OBS_BLOCK), F), last], 0).astype(BF)
        ones = jnp.where(lax.broadcasted_iota(jnp.int32, (SRC - 64, OBS_BLOCK), 0) == 0, 1.0, 0.0)
        v = jnp.concatenate([vals[:, ks].astype(F), ones], 0)
        for p in range(ROWS):
            scaled[p * SRC:(p + 1) * SRC] = (v * lat_weight[p:p + 1]).astype(BF)
        for m in range(0, ROWS * SRC, 640):
            acc[m:m + 640] += lax.dot_general(
                scaled[m:m + 640], lon_weight, (((1,), (1,)), ((), ())), preferred_element_type=F)
        return 0

    lax.fori_loop(0, (live_count + OBS_BLOCK - 1) // OBS_BLOCK, add_block, 0)
    for copy in copies[3:]:
        copy.wait()
    for p in range(ROWS):
        sums[p] = acc[p * SRC:(p + 1) * SRC].astype(BF)
    def fill(up, down):
        for msg, first, state_tile, state_row in ((up, 0, 0, 0), (down, 24, 8, 5)):
            side = jnp.zeros((SRC, 128), F)
            for i in range(8):
                part = acc[(first + i) * SRC:(first + i + 1) * SRC]
                msg[i * SRC:(i + 1) * SRC] = part[:, :128].astype(BF)
                moved = pltpu.roll(part[:, 128:], i * 8 + 4, 1)
                side = jnp.where((lanes(SRC) >> 3) == i, moved, side)
            msg[8 * SRC:9 * SRC] = side.astype(BF)
            for c in range(0, 256, 16):
                x = jnp.swapaxes(state[c:c + 16, state_tile:state_tile + 8, :].astype(F), 0, 1).astype(BF)
                for j in range(3):
                    msg[LAT_STATE + j * 256 + c:LAT_STATE + j * 256 + c + 16] = x[state_row + j]

    @pl.when(even(lat))
    def _():
        fill(out_b, out_a)

    @pl.when(jnp.logical_not(even(lat)))
    def _():
        fill(out_a, out_b)


def observation_sums(obs_values, obs_offsets, obs_cell, obs_count, lat, state):
    S = pl.BlockSpec(memory_space=pltpu.SMEM)
    V = pl.BlockSpec(memory_space=pltpu.VMEM)
    shape = jax.ShapeDtypeStruct
    return pl.pallas_call(
        sums_kernel, name="observation_sums",
        out_shape=(shape((ROWS, SRC, 256), BF), shape((LAT_MSG, 128), BF), shape((LAT_MSG, 128), BF)),
        in_specs=[S, S] + [pl.BlockSpec(memory_space=pl.ANY)] * 4, out_specs=(V,) * 3,
        scratch_shapes=[
            pltpu.VMEM((64, 2048), BF), pltpu.VMEM((2, 2048), F), pltpu.VMEM((1, 2048), jnp.int32), pltpu.VMEM((256, 16, 128), BF),
            pltpu.VMEM((ROWS * SRC, OBS_BLOCK), BF), pltpu.VMEM((ROWS * SRC, 256), F), pltpu.SemaphoreType.DMA((5,)),
        ],
        compiler_params=pltpu.CompilerParams(vmem_limit_bytes=56 * MIB),
    )(obs_count, lat, obs_values, obs_offsets, obs_cell.reshape(1, -1), state)


def place(p):
    return 15 - p % 16


def pack(packed, p, main, side):
    lane = lanes(SRC)
    k, shift = p // 16, place(p) * 8 + 4
    here = (lane >> 3) == place(p)
    packed[0][k] = jnp.where(here, pltpu.roll(jnp.where(lane < 4, main, side), shift, 1), packed[0][k])
    packed[1][k] = jnp.where(here, pltpu.roll(jnp.where(lane >= 124, main, side), shift, 1), packed[1][k])


def rows_kernel(state, sums, rows, rims):
    def turn(i, _):
        c0 = pl.multiple_of(i * 16, 16)
        rows[:, pl.ds(c0, 16), :] = jnp.swapaxes(state[pl.ds(c0, 16)].astype(F), 0, 1).astype(BF)
        return 0

    lax.fori_loop(0, 16, turn, 0)
    for c in range(0, 256, 64):
        packed = [jnp.zeros((64, 128), F) for _ in range(2)]
        for r in range(24):
            p = r + W
            moved = pltpu.roll(rows[r, c:c + 64, :].astype(F), place(p) * 8 + 4, 1)
            packed[p // 16] = jnp.where((lanes(64) >> 3) == place(p), moved, packed[p // 16])
        for k in range(2):
            rims[LON_STATE + k * 256 + c:LON_STATE + k * 256 + c + 64] = packed[k].astype(BF)
    packed = [[jnp.zeros((SRC, 128), F) for _ in range(2)] for _ in range(2)]
    for p in range(8, 24):
        pack(packed, p, sums[p, :, :128].astype(F), sums[p, :, 128:].astype(F))
    for k in range(2):
        rims[k * SRC:(k + 1) * SRC] = packed[0][k].astype(BF)
        rims[RIMS + k * SRC:RIMS + (k + 1) * SRC] = packed[1][k].astype(BF)


def state_rows(state, sums):
    shape = jax.ShapeDtypeStruct
    return pl.pallas_call(
        rows_kernel, name="state_rows", out_shape=(shape((24, 256, 128), BF), shape((RIMS + LON_STATE, 128), BF)),
        cost_estimate=pl.CostEstimate(flops=10**7, bytes_accessed=8 * 10**6, transcendentals=0),
        compiler_params=pltpu.CompilerParams(vmem_limit_bytes=16 * MIB),
    )(state, sums)


def edge_kernel(lat, lon, sums, rims, in_a, in_b, edge, out_a, out_b):
    lat_even, lon_even = even(lat), even(lon)
    above = lambda at: pick(lat_even, in_b, in_a, at)
    below = lambda at: pick(lat_even, in_a, in_b, at)

    def store(at, left, right):
        out_a[at] = jnp.where(lon_even, right, left).astype(BF)
        out_b[at] = jnp.where(lon_even, left, right).astype(BF)

    lane = lanes(SRC)
    outer = (lane < 4) | (lane >= 124)
    packed = [[rims[first + k * SRC:first + (k + 1) * SRC].astype(F) for k in range(2)] for first in (0, RIMS)]
    for e in range(16):
        p = e if e < 8 else e + 16
        msg, i = (above, p) if p < 8 else (below, p - 24)
        moved = pltpu.roll(msg(slice(8 * SRC, 9 * SRC)), 124 - i * 8, 1)
        main = sums[p, :, :128].astype(F) + msg(slice(i * SRC, (i + 1) * SRC))
        side = sums[p, :, 128:].astype(F) + jnp.where(outer, moved, 0.0)
        edge[e] = main.astype(BF)
        pack(packed, p, main, side)
    for k in range(2):
        store(slice(k * SRC, (k + 1) * SRC), packed[0][k], packed[1][k])
    early = (lanes(64) & 7) < 4
    for c in range(0, 256, 64):
        halves = []
        for k, msg, first in ((0, above, 1), (1, below, 28)):
            at = LON_STATE + k * 256 + c
            out = rims[at:at + 64].astype(F)
            for j in range(3):
                p = first + j
                x = msg(slice(LAT_STATE + j * 256 + c, LAT_STATE + j * 256 + c + 64))
                out = jnp.where((lanes(64) >> 3) == place(p), pltpu.roll(x, place(p) * 8 + 4, 1), out)
            halves.append(out)
        at = slice(LON_STATE + c, LON_STATE + c + 64)
        store(
            at,
            jnp.where(early, pltpu.roll(halves[1], 124, 1), halves[0]),
            jnp.where(early, halves[0], pltpu.roll(halves[1], 4, 1)),
        )


def edge_sums(*arrays):
    shape = jax.ShapeDtypeStruct
    return pl.pallas_call(
        edge_kernel, name="edge_sums", in_specs=[pl.BlockSpec(memory_space=pltpu.SMEM)] * 2 + [pl.BlockSpec(memory_space=pltpu.VMEM)] * 4,
        out_shape=(shape((16, SRC, 128), BF), shape((LON_MSG, 128), BF), shape((LON_MSG, 128), BF)),
        compiler_params=pltpu.CompilerParams(vmem_limit_bytes=16 * MIB),
    )(*arrays)


def prepare_kernel(taps, w_in, w_up, w_down, b1, toe, wi, w1, w2, b1c, smat, padded, base):
    smat[...] = shift_matrix()
    padded[...] = jnp.zeros(padded.shape, F)
    padded[0:65] = w_in[...].astype(F)
    wi[...] = padded[...].T.astype(BF)
    w1[...] = w_up[...].T
    w2[...] = w_down[...].T
    b1c[...] = b1[...].T
    base[...] = jnp.zeros(base.shape, F)
    for v in range(7):
        for u in range(7):
            base[32 * v + 1 + u:32 * v + 2 + u] = taps[u, v:v + 1]
    base[...] = base[...].T

    def step(i, _):
        rows = base[pl.ds(pl.multiple_of(i * 8, 8), 8), :]
        for k in range(8):
            parts = []
            for ln in range(2):
                b = jnp.broadcast_to(rows[k:k + 1, ln * 128:(ln + 1) * 128], (24, 128))
                parts.append(pltpu.roll(b, 0, 1, stride=1, stride_axis=0))
            y = jnp.concatenate(parts, 1).astype(BF)
            toe[i * 4 + k // 2, (k % 2) * 24:(k % 2) * 24 + 24, :] = y[:, :224]
        return 0

    lax.fori_loop(0, 32, step, 0)


def prepare(dw_weight, w_in, w_up, w_down, up_bias):
    shape = jax.ShapeDtypeStruct
    return pl.pallas_call(
        prepare_kernel, name="prepare",
        out_shape=(shape((128, 48, 224), BF), shape((256, SRC), BF), shape((1024, 256), BF), shape((256, 1024), BF), shape((128, 8), F), shape((256, 768), BF)),
        scratch_shapes=[pltpu.VMEM((SRC, 256), F), pltpu.VMEM((256, 256), F)],
        cost_estimate=pl.CostEstimate(flops=10**7, bytes_accessed=8 * 10**6, transcendentals=0),
        compiler_params=pltpu.CompilerParams(vmem_limit_bytes=16 * MIB),
    )(jnp.transpose(dw_weight, (1, 2, 0)), w_in, w_up, w_down, up_bias.reshape(8, 128))


def shift_matrix():
    lane = lax.broadcasted_iota(jnp.int32, (256, 768), 0)
    out = lax.broadcasted_iota(jnp.int32, (256, 768), 1)
    j = lane & 7
    col = jnp.where(lane < 128, lane, jnp.where(j < 4, j - 4, j + 124))
    k = out // 128
    d = jnp.where(k < 3, k - 3, k - 2)
    return jnp.where(col == out % 128 + d, 1.0, 0.0).astype(BF)


def encode_kernel(lat, sums, edge, in_a, in_b, rows, wi, native, mixed):
    lat_even = even(lat)

    def encode(*cases):
        both = jnp.dot(wi[...], jnp.concatenate([main for _, main, _ in cases], 1), preferred_element_type=F)
        for n, (p, _, state) in enumerate(cases):
            mixed[p] = (both[:, n * 128:(n + 1) * 128] + state.astype(F)).astype(BF)

    mixed[0] = jnp.zeros((256, 128), BF)
    mixed[31] = jnp.zeros((256, 128), BF)
    for j in range(3):
        at = slice(LAT_STATE + j * 256, LAT_STATE + j * 256 + 256)
        encode((1 + j, edge[1 + j], pick(lat_even, in_b, in_a, at)), (28 + j, edge[12 + j], pick(lat_even, in_a, in_b, at)))

    def edge_row(j, _):
        encode((4 + j, edge[4 + j], rows[j]), (24 + j, edge[8 + j], rows[20 + j]))
        return 0

    def inner_row(j, _):
        encode((8 + j, sums[8 + j, :, :128], rows[4 + j]), (16 + j, sums[16 + j, :, :128], rows[12 + j]))
        return 0

    lax.fori_loop(0, 4, edge_row, 0)
    lax.fori_loop(0, 8, inner_row, 0)

    def turn(i, _):
        c0 = pl.multiple_of(i * CB, CB)
        native[pl.ds(c0, CB)] = jnp.swapaxes(mixed[:, pl.ds(c0, CB), :].astype(F), 0, 1).astype(BF)
        return 0

    lax.fori_loop(0, 256 // CB, turn, 0)


def encode(*arrays):
    return pl.pallas_call(
        encode_kernel, name="encode", in_specs=[pl.BlockSpec(memory_space=pltpu.SMEM)] + [pl.BlockSpec(memory_space=pltpu.VMEM)] * 6,
        out_shape=jax.ShapeDtypeStruct((256, ROWS, 128), BF),
        scratch_shapes=[pltpu.VMEM((ROWS, 256, 128), BF)],
        cost_estimate=pl.CostEstimate(flops=10**8, bytes_accessed=8 * 10**6, transcendentals=0),
        compiler_params=pltpu.CompilerParams(vmem_limit_bytes=20 * MIB),
    )(*arrays)


def block_kernel(lon, dwb, gain, nbias, db, ls, partial, out_a, out_b, in_a, in_b,
                 toe, wi, w1, b1, w2, smat, out, native, sides, inward, mext, xs, filt, xbuf, obuf, result, sems):
    lon_even = even(lon)
    first = (lanes(SRC) & 7) < 4
    parts = []
    for k in range(2):
        at = slice(k * SRC, (k + 1) * SRC)
        a, b = pick(lon_even, in_b, in_a, at), pick(lon_even, in_a, in_b, at)
        parts.append(jnp.where(first, pick(lon_even, out_b, out_a, at) + a, pick(lon_even, out_a, out_b, at) + b))
        parts.append(jnp.where(first, b, a))
    both = jnp.dot(wi[...], jnp.concatenate(parts, 1).astype(BF), preferred_element_type=F)
    first = (lanes(256) & 7) < 4
    at = slice(LON_STATE, LON_STATE + 256)
    a, b = pick(lon_even, in_b, in_a, at), pick(lon_even, in_a, in_b, at)
    rims = (jnp.where(first, a, b), jnp.where(first, pltpu.roll(a, 124, 1), pltpu.roll(b, 4, 1)))
    for k in range(2):
        sides[:, k * 128:(k + 1) * 128] = (both[:, 2 * k * 128:(2 * k + 1) * 128] + rims[k]).astype(BF).astype(F)
        inward[:, k * 128:(k + 1) * 128] = both[:, (2 * k + 1) * 128:(2 * k + 2) * 128]
    slot = (lanes(16) >> 3) == 15 - lax.broadcasted_iota(jnp.int32, (16, 128), 0)
    outer = (lanes(16) < 4) | (lanes(16) >= 124)

    def filt_step(i, carry):
        pivot, s1, s2 = carry
        c0 = pl.multiple_of(i * CB, CB)
        side, more = sides[pl.ds(c0, CB)], inward[pl.ds(c0, CB)]
        for c in range(CB):
            for k in range(2):
                at = slice(c * 32 + k * 16, c * 32 + k * 16 + 16)
                ks = slice(k * 128, (k + 1) * 128)
                spread = jnp.broadcast_to(side[c:c + 1, ks], (16, 128))
                mext[at, 128:] = jnp.where(slot, spread, 0.0).astype(BF)
                moved = pltpu.roll(jnp.broadcast_to(more[c:c + 1, ks], (16, 128)), 4, 1, stride=8, stride_axis=0)
                main = (partial[c0 + c, k * 16:k * 16 + 16].astype(F) + jnp.where(outer, moved, 0.0)).astype(BF)
                mext[at, :128] = main
                native[c0 + c, k * 16:k * 16 + 16] = main
                xs[c // 2, 96 + k * 16:112 + k * 16, (c % 2) * 128:(c % 2) * 128 + 128] = main
        for j in range(3):
            z = jnp.dot(mext[...], smat[:, j * 256:(j + 1) * 256], preferred_element_type=F).astype(BF)
            for half in range(2):
                k = 2 * j + half
                v = k if k < 3 else k + 1
                zz = z[:, half * 128:(half + 1) * 128]
                for c in range(CB):
                    xs[c // 2, v * 32:(v + 1) * 32, (c % 2) * 128:(c % 2) * 128 + 128] = zz[c * 32:(c + 1) * 32]
        for k in range(CB // 2):
            o = jnp.dot(toe[i * (CB // 2) + k], xs[k], preferred_element_type=F)
            for c, y in ((c0 + 2 * k, o[:24, :128]), (c0 + 2 * k + 1, o[24:, 128:])):
                y = y + dwb[c]
                if k == 0:
                    pivot = jnp.where(c == 0, y, pivot)
                y = y - pivot
                filt[c] = y
                s1 = s1 + y
                s2 = s2 + y * y
        return pivot, s1, s2

    zero = jnp.zeros((24, 128), F)
    _, s1, s2 = lax.fori_loop(0, 256 // CB, filt_step, (zero, zero, zero))
    mean = s1 * (1.0 / 256)
    rstd = lax.rsqrt(jnp.maximum(s2 * (1.0 / 256) - mean * mean, 0.0) + 1e-6)

    def norm_step(i, _):
        c0 = pl.multiple_of(i * 16, 16)
        ys = [((filt[c0 + k] - mean) * rstd) * gain[c0 + k] + nbias[c0 + k] for k in range(16)]
        xbuf[:, pl.ds(c0, 16), :] = jnp.swapaxes(jnp.stack(ys, 0), 0, 1).astype(BF)
        return 0

    lax.fori_loop(0, 16, norm_step, 0)

    def mlp_step(i, _):
        x = jnp.concatenate([xbuf[i * RB + k] for k in range(RB)], 1)
        h = jnp.dot(w1[...], x, preferred_element_type=F)
        gs = []
        for k in range(8):
            hk = h[k * 128:(k + 1) * 128] + b1[:, k:k + 1]
            gs.append(((0.5 * hk) * (1.0 + lax.erf(hk * 0.7071067811865476))).astype(BF))
        o = jnp.dot(w2[...], jnp.concatenate(gs, 0), preferred_element_type=F)
        for k in range(RB):
            obuf[i * RB + k] = o[:, k * 128:(k + 1) * 128]
        return 0

    lax.fori_loop(0, 24 // RB, mlp_step, 0, unroll=3)

    def out_step(i, _):
        c0 = pl.multiple_of(i * 16, 16)
        o = jnp.swapaxes(obuf[:, pl.ds(c0, 16), :], 0, 1)
        m = native[pl.ds(c0, 16)].astype(F)
        for k in range(16):
            result[c0 + k] = (m[k, 4:28] + (o[k] + db[c0 + k]) * ls[c0 + k]).astype(BF)
        return 0

    copies = []
    for n in range(4):
        lax.fori_loop(4 * n, 4 * n + 4, out_step, 0)
        at = slice(64 * n, 64 * n + 64)
        copies.append(pltpu.make_async_copy(result.at[at], out.at[at], sems.at[n]))
        copies[-1].start()
    for copy in copies:
        copy.wait()


def block(arrays, vectors):
    S = pl.BlockSpec(memory_space=pltpu.SMEM)
    V = pl.BlockSpec(memory_space=pltpu.VMEM)
    return pl.pallas_call(
        block_kernel, name="block", out_shape=jax.ShapeDtypeStruct((256, 24, 128), BF),
        in_specs=[S] * len(vectors) + [V] * len(arrays), out_specs=pl.BlockSpec(memory_space=pl.ANY),
        scratch_shapes=[
            pltpu.VMEM((256, ROWS, 128), BF), pltpu.VMEM((256, 256), F), pltpu.VMEM((256, 256), F),
            pltpu.VMEM((CB * 32, 256), BF), pltpu.VMEM((CB // 2, 224, 256), BF),
            pltpu.VMEM((256, 24, 128), F), pltpu.VMEM((24, 256, 128), BF), pltpu.VMEM((24, 256, 128), F),
            pltpu.VMEM((256, 24, 128), BF), pltpu.SemaphoreType.DMA((4,)),
        ],
        compiler_params=pltpu.CompilerParams(vmem_limit_bytes=30 * MIB),
    )(*vectors, *arrays)


def exchange(a, b, axis, wrap):
    size = lax.axis_size(axis)
    first = [(i, i + 1) for i in range(0, size, 2)]
    second = [(i, (i + 1) % size) for i in range(1, size if wrap else size - 1, 2)]
    swap = lambda x, pairs: lax.ppermute(x, axis, pairs + [(j, i) for i, j in pairs])
    return swap(a, first), swap(b, second)


def local(state, obs_values, obs_offsets, obs_cell, obs_count, w_in, dw_weight, dw_bias, norm_gain, norm_bias,
          w_up, up_bias, w_down, down_bias, layer_scale):
    lat = lax.axis_index("lat").astype(jnp.int32).reshape(1)
    lon = lax.axis_index("lon").astype(jnp.int32).reshape(1)
    sums, lat_a, lat_b = observation_sums(obs_values, obs_offsets, obs_cell, obs_count, lat, state)
    lat_a, lat_b = exchange(lat_a, lat_b, "lat", False)
    rows, rims = state_rows(state, sums)
    dw_later, w_up_later, w_down_later, _ = lax.optimization_barrier((dw_weight, w_up, w_down, rows))
    weights = prepare(dw_later, w_in, w_up_later, w_down_later, up_bias)
    rims, (toe, wi, w1, w2, b1, smat) = lax.optimization_barrier((rims, weights))
    edge, lon_a, lon_b = edge_sums(lat, lon, sums, rims, lat_a, lat_b)
    from_a, from_b = exchange(lon_a, lon_b, "lon", True)
    partial = encode(lat, sums, edge, lat_a, lat_b, rows, wi)
    return block(
        (partial, lon_a, lon_b, from_a, from_b, toe, wi, w1, b1, w2, smat),
        (lon, dw_bias, norm_gain, norm_bias, down_bias, layer_scale),
    )


def solution(mesh):
    return jax.shard_map(
        local,
        mesh=mesh,
        in_specs=(
            P(None, "lat", "lon"),
            P(None, ("lat", "lon")),
            P(None, ("lat", "lon")),
            P(("lat", "lon")),
            P(("lat", "lon")),
            P(),
            P(),
            P(),
            P(),
            P(),
            P(),
            P(),
            P(),
            P(),
            P(),
        ),
        out_specs=P(None, "lat", "lon"),
        check_vma=False,
    )
```

```python
import jax
import jax.numpy as jnp
from jax import lax
from jax.experimental import pallas as pl
from jax.experimental.pallas import tpu as pltpu
from jax.sharding import PartitionSpec as P

W = 4
SRC = 80
ROWS = 32
OBS_BLOCK = 512
GRID_ROWS = 384
CB = 128
RB = 8
BF = jnp.bfloat16
F = jnp.float32
MIB = 2**20
LAT_STATE = 9 * SRC
LAT_MSG = 9 * SRC + 3 * 256
LON_STATE = 2 * SRC
LON_MSG = 2 * SRC + 256
RIMS = 2 * SRC + 2 * 256

inverse_width = 1.0 / (2.0 * 1.5 * 1.5)


def lanes(rows):
    return lax.broadcasted_iota(jnp.int32, (rows, 128), 1)


def even(index):
    return (index[0] & 1) == 0


def pick(condition, a, b, at):
    return jnp.where(condition, a[at].astype(F), b[at].astype(F))


def sums_kernel(count, lat, vals_in, offs_in, cell_in, state_in, sums, out_a, out_b, vals, offs, cell, state, scaled, acc, sems):
    live_count = count[0]
    row_base = lat[0] * 24
    copies = [
        pltpu.make_async_copy(vals_in, vals, sems.at[0]),
        pltpu.make_async_copy(offs_in, offs, sems.at[1]),
        pltpu.make_async_copy(cell_in, cell, sems.at[2]),
        pltpu.make_async_copy(state_in.at[:, 0:8, :], state.at[:, 0:8, :], sems.at[3]),
        pltpu.make_async_copy(state_in.at[:, 16:24, :], state.at[:, 8:16, :], sems.at[4]),
    ]
    for copy in copies:
        copy.start()
    acc[...] = jnp.zeros(acc.shape, F)
    for copy in copies[:3]:
        copy.wait()

    def add_block(b, _):
        k0 = pl.multiple_of(b * OBS_BLOCK, OBS_BLOCK)
        ks = pl.ds(k0, OBS_BLOCK)
        where_cell = cell[:, ks]
        row = where_cell >> 7
        col = where_cell & 127
        slot = lax.broadcasted_iota(jnp.int32, (1, OBS_BLOCK), 1) + k0
        row = jnp.where(slot < live_count, row, -100)

        def weight(offset, place, centre, valid):
            apart = place - centre
            spread = offset - apart.astype(F) - 0.5
            inside = (jnp.abs(apart) <= W) & valid
            return jnp.where(inside, jnp.exp(-spread * spread * inverse_width), 0.0)

        place = lax.broadcasted_iota(jnp.int32, (ROWS, OBS_BLOCK), 0) - W
        on_grid = (place + row_base >= 0) & (place + row_base < GRID_ROWS)
        lat_weight = weight(offs[0:1, ks], place, row, on_grid)
        place = lax.broadcasted_iota(jnp.int32, (136, OBS_BLOCK), 0)
        first = weight(offs[1:2, ks], place, col, place < 128 + W)
        place = lax.broadcasted_iota(jnp.int32, (8, OBS_BLOCK), 0) - 8
        last = weight(offs[1:2, ks], place, col, place >= -W)
        lon_weight = jnp.concatenate([first, jnp.zeros((112, OBS_BLOCK), F), last], 0).astype(BF)
        ones = jnp.where(lax.broadcasted_iota(jnp.int32, (SRC - 64, OBS_BLOCK), 0) == 0, 1.0, 0.0)
        v = jnp.concatenate([vals[:, ks].astype(F), ones], 0)
        for p in range(ROWS):
            scaled[p * SRC:(p + 1) * SRC] = (v * lat_weight[p:p + 1]).astype(BF)
        for m in range(0, ROWS * SRC, 640):
            acc[m:m + 640] += lax.dot_general(
                scaled[m:m + 640], lon_weight, (((1,), (1,)), ((), ())), preferred_element_type=F)
        return 0

    lax.fori_loop(0, (live_count + OBS_BLOCK - 1) // OBS_BLOCK, add_block, 0)
    for copy in copies[3:]:
        copy.wait()
    for p in range(ROWS):
        sums[p] = acc[p * SRC:(p + 1) * SRC].astype(BF)
    def fill(up, down):
        for msg, first, state_tile, state_row in ((up, 0, 0, 0), (down, 24, 8, 5)):
            side = jnp.zeros((SRC, 128), F)
            for i in range(8):
                part = acc[(first + i) * SRC:(first + i + 1) * SRC]
                msg[i * SRC:(i + 1) * SRC] = part[:, :128].astype(BF)
                moved = pltpu.roll(part[:, 128:], i * 8 + 4, 1)
                side = jnp.where((lanes(SRC) >> 3) == i, moved, side)
            msg[8 * SRC:9 * SRC] = side.astype(BF)
            for c in range(0, 256, 16):
                x = jnp.swapaxes(state[c:c + 16, state_tile:state_tile + 8, :].astype(F), 0, 1).astype(BF)
                for j in range(3):
                    msg[LAT_STATE + j * 256 + c:LAT_STATE + j * 256 + c + 16] = x[state_row + j]

    @pl.when(even(lat))
    def _():
        fill(out_b, out_a)

    @pl.when(jnp.logical_not(even(lat)))
    def _():
        fill(out_a, out_b)


def observation_sums(obs_values, obs_offsets, obs_cell, obs_count, lat, state):
    S = pl.BlockSpec(memory_space=pltpu.SMEM)
    V = pl.BlockSpec(memory_space=pltpu.VMEM)
    shape = jax.ShapeDtypeStruct
    return pl.pallas_call(
        sums_kernel, name="observation_sums",
        out_shape=(shape((ROWS, SRC, 256), BF), shape((LAT_MSG, 128), BF), shape((LAT_MSG, 128), BF)),
        in_specs=[S, S] + [pl.BlockSpec(memory_space=pl.ANY)] * 4, out_specs=(V,) * 3,
        scratch_shapes=[
            pltpu.VMEM((64, 2048), BF), pltpu.VMEM((2, 2048), F), pltpu.VMEM((1, 2048), jnp.int32), pltpu.VMEM((256, 16, 128), BF),
            pltpu.VMEM((ROWS * SRC, OBS_BLOCK), BF), pltpu.VMEM((ROWS * SRC, 256), F), pltpu.SemaphoreType.DMA((5,)),
        ],
        compiler_params=pltpu.CompilerParams(vmem_limit_bytes=56 * MIB),
    )(obs_count, lat, obs_values, obs_offsets, obs_cell.reshape(1, -1), state)


def place(p):
    return 15 - p % 16


def pack(packed, p, main, side):
    lane = lanes(SRC)
    k, shift = p // 16, place(p) * 8 + 4
    here = (lane >> 3) == place(p)
    packed[0][k] = jnp.where(here, pltpu.roll(jnp.where(lane < 4, main, side), shift, 1), packed[0][k])
    packed[1][k] = jnp.where(here, pltpu.roll(jnp.where(lane >= 124, main, side), shift, 1), packed[1][k])


def rows_kernel(state, sums, rows, rims):
    def turn(i, _):
        c0 = pl.multiple_of(i * 16, 16)
        rows[:, pl.ds(c0, 16), :] = jnp.swapaxes(state[pl.ds(c0, 16)].astype(F), 0, 1).astype(BF)
        return 0

    lax.fori_loop(0, 16, turn, 0)
    for c in range(0, 256, 64):
        packed = [jnp.zeros((64, 128), F) for _ in range(2)]
        for r in range(24):
            p = r + W
            moved = pltpu.roll(rows[r, c:c + 64, :].astype(F), place(p) * 8 + 4, 1)
            packed[p // 16] = jnp.where((lanes(64) >> 3) == place(p), moved, packed[p // 16])
        for k in range(2):
            rims[LON_STATE + k * 256 + c:LON_STATE + k * 256 + c + 64] = packed[k].astype(BF)
    packed = [[jnp.zeros((SRC, 128), F) for _ in range(2)] for _ in range(2)]
    for p in range(8, 24):
        pack(packed, p, sums[p, :, :128].astype(F), sums[p, :, 128:].astype(F))
    for k in range(2):
        rims[k * SRC:(k + 1) * SRC] = packed[0][k].astype(BF)
        rims[RIMS + k * SRC:RIMS + (k + 1) * SRC] = packed[1][k].astype(BF)


def state_rows(state, sums):
    shape = jax.ShapeDtypeStruct
    return pl.pallas_call(
        rows_kernel, name="state_rows", out_shape=(shape((24, 256, 128), BF), shape((RIMS + LON_STATE, 128), BF)),
        cost_estimate=pl.CostEstimate(flops=10**7, bytes_accessed=8 * 10**6, transcendentals=0),
        compiler_params=pltpu.CompilerParams(vmem_limit_bytes=16 * MIB),
    )(state, sums)


def edge_kernel(lat, lon, sums, rims, in_a, in_b, edge, out_a, out_b):
    lat_even, lon_even = even(lat), even(lon)
    above = lambda at: pick(lat_even, in_b, in_a, at)
    below = lambda at: pick(lat_even, in_a, in_b, at)

    def store(at, left, right):
        out_a[at] = jnp.where(lon_even, right, left).astype(BF)
        out_b[at] = jnp.where(lon_even, left, right).astype(BF)

    lane = lanes(SRC)
    outer = (lane < 4) | (lane >= 124)
    packed = [[rims[first + k * SRC:first + (k + 1) * SRC].astype(F) for k in range(2)] for first in (0, RIMS)]
    for e in range(16):
        p = e if e < 8 else e + 16
        msg, i = (above, p) if p < 8 else (below, p - 24)
        moved = pltpu.roll(msg(slice(8 * SRC, 9 * SRC)), 124 - i * 8, 1)
        main = sums[p, :, :128].astype(F) + msg(slice(i * SRC, (i + 1) * SRC))
        side = sums[p, :, 128:].astype(F) + jnp.where(outer, moved, 0.0)
        edge[e] = main.astype(BF)
        pack(packed, p, main, side)
    for k in range(2):
        store(slice(k * SRC, (k + 1) * SRC), packed[0][k], packed[1][k])
    early = (lanes(64) & 7) < 4
    for c in range(0, 256, 64):
        halves = []
        for k, msg, first in ((0, above, 1), (1, below, 28)):
            at = LON_STATE + k * 256 + c
            out = rims[at:at + 64].astype(F)
            for j in range(3):
                p = first + j
                x = msg(slice(LAT_STATE + j * 256 + c, LAT_STATE + j * 256 + c + 64))
                out = jnp.where((lanes(64) >> 3) == place(p), pltpu.roll(x, place(p) * 8 + 4, 1), out)
            halves.append(out)
        at = slice(LON_STATE + c, LON_STATE + c + 64)
        store(
            at,
            jnp.where(early, pltpu.roll(halves[1], 124, 1), halves[0]),
            jnp.where(early, halves[0], pltpu.roll(halves[1], 4, 1)),
        )


def edge_sums(*arrays):
    shape = jax.ShapeDtypeStruct
    return pl.pallas_call(
        edge_kernel, name="edge_sums", in_specs=[pl.BlockSpec(memory_space=pltpu.SMEM)] * 2 + [pl.BlockSpec(memory_space=pltpu.VMEM)] * 4,
        out_shape=(shape((16, SRC, 128), BF), shape((LON_MSG, 128), BF), shape((LON_MSG, 128), BF)),
        compiler_params=pltpu.CompilerParams(vmem_limit_bytes=16 * MIB),
    )(*arrays)


def prepare_kernel(taps, w_in, w_up, w_down, b1, toe, wi, w1, w2, b1c, smat, padded, base):
    smat[...] = shift_matrix()
    padded[...] = jnp.zeros(padded.shape, F)
    padded[0:65] = w_in[...].astype(F)
    wi[...] = padded[...].T.astype(BF)
    w1[...] = w_up[...].T
    w2[...] = w_down[...].T
    b1c[...] = b1[...].T
    base[...] = jnp.zeros(base.shape, F)
    for v in range(7):
        for u in range(7):
            base[32 * v + 1 + u:32 * v + 2 + u] = taps[u, v:v + 1]
    base[...] = base[...].T

    def step(i, _):
        rows = base[pl.ds(pl.multiple_of(i * 8, 8), 8), :]
        for k in range(8):
            parts = []
            for ln in range(2):
                b = jnp.broadcast_to(rows[k:k + 1, ln * 128:(ln + 1) * 128], (24, 128))
                parts.append(pltpu.roll(b, 0, 1, stride=1, stride_axis=0))
            y = jnp.concatenate(parts, 1).astype(BF)
            toe[i * 4 + k // 2, (k % 2) * 24:(k % 2) * 24 + 24, :] = y[:, :224]
        return 0

    lax.fori_loop(0, 32, step, 0, unroll=4)


def prepare(dw_weight, w_in, w_up, w_down, up_bias):
    shape = jax.ShapeDtypeStruct
    return pl.pallas_call(
        prepare_kernel, name="prepare",
        out_shape=(shape((128, 48, 224), BF), shape((256, SRC), BF), shape((1024, 256), BF), shape((256, 1024), BF), shape((128, 8), F), shape((256, 768), BF)),
        scratch_shapes=[pltpu.VMEM((SRC, 256), F), pltpu.VMEM((256, 256), F)],
        cost_estimate=pl.CostEstimate(flops=10**7, bytes_accessed=8 * 10**6, transcendentals=0),
        compiler_params=pltpu.CompilerParams(vmem_limit_bytes=16 * MIB),
    )(jnp.transpose(dw_weight, (1, 2, 0)), w_in, w_up, w_down, up_bias.reshape(8, 128))


def shift_matrix():
    lane = lax.broadcasted_iota(jnp.int32, (256, 768), 0)
    out = lax.broadcasted_iota(jnp.int32, (256, 768), 1)
    j = lane & 7
    col = jnp.where(lane < 128, lane, jnp.where(j < 4, j - 4, j + 124))
    k = out // 128
    d = jnp.where(k < 3, k - 3, k - 2)
    return jnp.where(col == out % 128 + d, 1.0, 0.0).astype(BF)


def encode_kernel(lat, sums, edge, in_a, in_b, rows, wi, native, mixed):
    lat_even = even(lat)

    def encode(*cases):
        both = jnp.dot(wi[...], jnp.concatenate([main for _, main, _ in cases], 1), preferred_element_type=F)
        for n, (p, _, state) in enumerate(cases):
            mixed[p] = (both[:, n * 128:(n + 1) * 128] + state.astype(F)).astype(BF)

    mixed[0] = jnp.zeros((256, 128), BF)
    mixed[31] = jnp.zeros((256, 128), BF)
    for j in range(3):
        at = slice(LAT_STATE + j * 256, LAT_STATE + j * 256 + 256)
        encode((1 + j, edge[1 + j], pick(lat_even, in_b, in_a, at)), (28 + j, edge[12 + j], pick(lat_even, in_a, in_b, at)))

    def edge_row(j, _):
        encode((4 + j, edge[4 + j], rows[j]), (24 + j, edge[8 + j], rows[20 + j]))
        return 0

    def inner_row(j, _):
        encode((8 + j, sums[8 + j, :, :128], rows[4 + j]), (16 + j, sums[16 + j, :, :128], rows[12 + j]))
        return 0

    lax.fori_loop(0, 4, edge_row, 0, unroll=4)
    lax.fori_loop(0, 8, inner_row, 0, unroll=4)

    def turn(i, _):
        c0 = pl.multiple_of(i * CB, CB)
        native[pl.ds(c0, CB)] = jnp.swapaxes(mixed[:, pl.ds(c0, CB), :].astype(F), 0, 1).astype(BF)
        return 0

    lax.fori_loop(0, 256 // CB, turn, 0)


def encode(*arrays):
    return pl.pallas_call(
        encode_kernel, name="encode", in_specs=[pl.BlockSpec(memory_space=pltpu.SMEM)] + [pl.BlockSpec(memory_space=pltpu.VMEM)] * 6,
        out_shape=jax.ShapeDtypeStruct((256, ROWS, 128), BF),
        scratch_shapes=[pltpu.VMEM((ROWS, 256, 128), BF)],
        cost_estimate=pl.CostEstimate(flops=10**8, bytes_accessed=8 * 10**6, transcendentals=0),
        compiler_params=pltpu.CompilerParams(vmem_limit_bytes=20 * MIB),
    )(*arrays)


def block_kernel(lon, dwb, gain, nbias, db, ls, partial, out_a, out_b, in_a, in_b,
                 toe, wi, w1, b1, w2, smat, out, native, sides, inward, mext, xs, filt, xbuf, obuf, result, sems):
    lon_even = even(lon)
    first = (lanes(SRC) & 7) < 4
    parts = []
    for k in range(2):
        at = slice(k * SRC, (k + 1) * SRC)
        a, b = pick(lon_even, in_b, in_a, at), pick(lon_even, in_a, in_b, at)
        parts.append(jnp.where(first, pick(lon_even, out_b, out_a, at) + a, pick(lon_even, out_a, out_b, at) + b))
        parts.append(jnp.where(first, b, a))
    both = jnp.dot(wi[...], jnp.concatenate(parts, 1).astype(BF), preferred_element_type=F)
    first = (lanes(256) & 7) < 4
    at = slice(LON_STATE, LON_STATE + 256)
    a, b = pick(lon_even, in_b, in_a, at), pick(lon_even, in_a, in_b, at)
    rims = (jnp.where(first, a, b), jnp.where(first, pltpu.roll(a, 124, 1), pltpu.roll(b, 4, 1)))
    for k in range(2):
        sides[:, k * 128:(k + 1) * 128] = (both[:, 2 * k * 128:(2 * k + 1) * 128] + rims[k]).astype(BF).astype(F)
        inward[:, k * 128:(k + 1) * 128] = both[:, (2 * k + 1) * 128:(2 * k + 2) * 128]
    slot = (lanes(16) >> 3) == 15 - lax.broadcasted_iota(jnp.int32, (16, 128), 0)
    outer = (lanes(16) < 4) | (lanes(16) >= 124)

    def filt_step(i, carry):
        pivot, s1, s2 = carry
        c0 = pl.multiple_of(i * CB, CB)
        side, more = sides[pl.ds(c0, CB)], inward[pl.ds(c0, CB)]
        for c in range(CB):
            for k in range(2):
                at = slice(c * 32 + k * 16, c * 32 + k * 16 + 16)
                ks = slice(k * 128, (k + 1) * 128)
                spread = jnp.broadcast_to(side[c:c + 1, ks], (16, 128))
                mext[at, 128:] = jnp.where(slot, spread, 0.0).astype(BF)
                moved = pltpu.roll(jnp.broadcast_to(more[c:c + 1, ks], (16, 128)), 4, 1, stride=8, stride_axis=0)
                main = (partial[c0 + c, k * 16:k * 16 + 16].astype(F) + jnp.where(outer, moved, 0.0)).astype(BF)
                mext[at, :128] = main
                native[c0 + c, k * 16:k * 16 + 16] = main
                xs[c // 2, 96 + k * 16:112 + k * 16, (c % 2) * 128:(c % 2) * 128 + 128] = main
        for j in range(3):
            z = jnp.dot(mext[...], smat[:, j * 256:(j + 1) * 256], preferred_element_type=F).astype(BF)
            for half in range(2):
                k = 2 * j + half
                v = k if k < 3 else k + 1
                zz = z[:, half * 128:(half + 1) * 128]
                for c in range(CB):
                    xs[c // 2, v * 32:(v + 1) * 32, (c % 2) * 128:(c % 2) * 128 + 128] = zz[c * 32:(c + 1) * 32]
        for k in range(CB // 2):
            o = jnp.dot(toe[i * (CB // 2) + k], xs[k], preferred_element_type=F)
            for c, y in ((c0 + 2 * k, o[:24, :128]), (c0 + 2 * k + 1, o[24:, 128:])):
                y = y + dwb[c]
                if k == 0:
                    pivot = jnp.where(c == 0, y, pivot)
                y = y - pivot
                filt[c] = y
                s1 = s1 + y
                s2 = s2 + y * y
        return pivot, s1, s2

    zero = jnp.zeros((24, 128), F)
    _, s1, s2 = lax.fori_loop(0, 256 // CB, filt_step, (zero, zero, zero))
    mean = s1 * (1.0 / 256)
    rstd = lax.rsqrt(jnp.maximum(s2 * (1.0 / 256) - mean * mean, 0.0) + 1e-6)

    def norm_step(i, _):
        c0 = pl.multiple_of(i * 16, 16)
        ys = [((filt[c0 + k] - mean) * rstd) * gain[c0 + k] + nbias[c0 + k] for k in range(16)]
        xbuf[:, pl.ds(c0, 16), :] = jnp.swapaxes(jnp.stack(ys, 0), 0, 1).astype(BF)
        return 0

    lax.fori_loop(0, 16, norm_step, 0, unroll=4)

    def mlp_step(i, _):
        x = jnp.concatenate([xbuf[i * RB + k] for k in range(RB)], 1)
        h = jnp.dot(w1[...], x, preferred_element_type=F)
        gs = []
        for k in range(8):
            hk = h[k * 128:(k + 1) * 128] + b1[:, k:k + 1]
            gs.append(((0.5 * hk) * (1.0 + lax.erf(hk * 0.7071067811865476))).astype(BF))
        o = jnp.dot(w2[...], jnp.concatenate(gs, 0), preferred_element_type=F)
        for k in range(RB):
            obuf[i * RB + k] = o[:, k * 128:(k + 1) * 128]
        return 0

    lax.fori_loop(0, 24 // RB, mlp_step, 0, unroll=3)

    def out_step(i, _):
        c0 = pl.multiple_of(i * 16, 16)
        o = jnp.swapaxes(obuf[:, pl.ds(c0, 16), :], 0, 1)
        m = native[pl.ds(c0, 16)].astype(F)
        for k in range(16):
            result[c0 + k] = (m[k, 4:28] + (o[k] + db[c0 + k]) * ls[c0 + k]).astype(BF)
        return 0

    copies = []
    for n in range(4):
        lax.fori_loop(4 * n, 4 * n + 4, out_step, 0, unroll=4)
        at = slice(64 * n, 64 * n + 64)
        copies.append(pltpu.make_async_copy(result.at[at], out.at[at], sems.at[n]))
        copies[-1].start()
    for copy in copies:
        copy.wait()


def block(arrays, vectors):
    S = pl.BlockSpec(memory_space=pltpu.SMEM)
    V = pl.BlockSpec(memory_space=pltpu.VMEM)
    return pl.pallas_call(
        block_kernel, name="block", out_shape=jax.ShapeDtypeStruct((256, 24, 128), BF),
        in_specs=[S] * len(vectors) + [V] * len(arrays), out_specs=pl.BlockSpec(memory_space=pl.ANY),
        scratch_shapes=[
            pltpu.VMEM((256, ROWS, 128), BF), pltpu.VMEM((256, 256), F), pltpu.VMEM((256, 256), F),
            pltpu.VMEM((CB * 32, 256), BF), pltpu.VMEM((CB // 2, 224, 256), BF),
            pltpu.VMEM((256, 24, 128), F), pltpu.VMEM((24, 256, 128), BF), pltpu.VMEM((24, 256, 128), F),
            pltpu.VMEM((256, 24, 128), BF), pltpu.SemaphoreType.DMA((4,)),
        ],
        compiler_params=pltpu.CompilerParams(vmem_limit_bytes=30 * MIB),
    )(*vectors, *arrays)


def exchange(a, b, axis, wrap):
    size = lax.axis_size(axis)
    first = [(i, i + 1) for i in range(0, size, 2)]
    second = [(i, (i + 1) % size) for i in range(1, size if wrap else size - 1, 2)]
    swap = lambda x, pairs: lax.ppermute(x, axis, pairs + [(j, i) for i, j in pairs])
    return swap(a, first), swap(b, second)


def local(state, obs_values, obs_offsets, obs_cell, obs_count, w_in, dw_weight, dw_bias, norm_gain, norm_bias,
          w_up, up_bias, w_down, down_bias, layer_scale):
    lat = lax.axis_index("lat").astype(jnp.int32).reshape(1)
    lon = lax.axis_index("lon").astype(jnp.int32).reshape(1)
    sums, lat_a, lat_b = observation_sums(obs_values, obs_offsets, obs_cell, obs_count, lat, state)
    lat_a, lat_b = exchange(lat_a, lat_b, "lat", False)
    rows, rims = state_rows(state, sums)
    dw_later, w_up_later, w_down_later, _ = lax.optimization_barrier((dw_weight, w_up, w_down, rows))
    weights = prepare(dw_later, w_in, w_up_later, w_down_later, up_bias)
    rims, (toe, wi, w1, w2, b1, smat) = lax.optimization_barrier((rims, weights))
    edge, lon_a, lon_b = edge_sums(lat, lon, sums, rims, lat_a, lat_b)
    from_a, from_b = exchange(lon_a, lon_b, "lon", True)
    partial = encode(lat, sums, edge, lat_a, lat_b, rows, wi)
    return block(
        (partial, lon_a, lon_b, from_a, from_b, toe, wi, w1, b1, w2, smat),
        (lon, dw_bias, norm_gain, norm_bias, down_bias, layer_scale),
    )


def solution(mesh):
    return jax.shard_map(
        local,
        mesh=mesh,
        in_specs=(
            P(None, "lat", "lon"),
            P(None, ("lat", "lon")),
            P(None, ("lat", "lon")),
            P(("lat", "lon")),
            P(("lat", "lon")),
            P(),
            P(),
            P(),
            P(),
            P(),
            P(),
            P(),
            P(),
            P(),
            P(),
        ),
        out_specs=P(None, "lat", "lon"),
        check_vma=False,
    )
```
